512 devices in a mesh: wide: 64 (over x, y, core), grp: 8 (over z).
Axes of the slice: x: 4, y: 8, z: 8, core: 2. Of those that a mesh axis runs over, the one named last changes fastest.
Arguments:
- dense_features: bfloat16 [65536, 128], P(('wide', 'grp')), may hold values from -6 to 6
- bag_slots: int32 [16, 65536, 8], P('grp', 'wide'), may hold values from 0 to 3071, as said below
- cold_offset: int32 [8, 64, 64, 16], P('grp', 'wide'), may hold values from -1 to 1023, as said below
- hot_rows: float32 [8, 2048, 128], P('grp'), may hold values from -2 to 2
- hot_accum: float32 [8, 2048], P('grp'), may hold values from 0.0001 to 0.01
- cold_rows: float32 [8, 65536, 128], P('grp', 'wide'), may hold values from -2 to 2
- cold_accum: float32 [8, 65536], P('grp', 'wide'), may hold values from 0.0001 to 0.01
- cross_down: bfloat16 [2176, 512], P('wide'), may hold values from -0.125 to 0.125
- cross_up: bfloat16 [512, 2176], P('wide'), may hold values from -0.25 to 0.25
- cross_bias: float32 [2176], replicated, may hold values from -3 to 3
- out_weight: bfloat16 [2176], replicated, may hold values from -0.125 to 0.125
- labels: int32 [65536], P(('wide', 'grp')), may hold values from 0 to 1
Outputs:
- logits: float32 [65536], P(('wide', 'grp'))
- new_hot_rows: float32 [8, 2048, 128], P('grp')
- new_hot_accum: float32 [8, 2048], P('grp')
- new_cold_rows: float32 [8, 65536, 128], P('grp', 'wide')
- new_cold_accum: float32 [8, 65536], P('grp', 'wide')
The draws below stay inside these ranges and needn't reach their ends.
Inputs may be any that keep to these rules, and one draw needn't show every extreme that they name: `bag_slots`: an entry below 2048 names a hot row of the group of its table; an entry 2048 + p * 16 + s names the row fetched by slot s of the request list of its block to owner p, and that slot is live. `cold_offset`: each list to one owner holds its live offsets first and -1 in the rest; some owner receives 16 live slots from every requester of its group.
All inputs are finite; a program needn't handle non-finite values.
Results may differ from the reference program's by a relative error of at most 0.0052.
Values may be sent and summed in bfloat16 or wider, within the bound.
A program may use at most 64 MiB of HBM per device.

```python
import math
import jax
import jax.numpy as jnp
from jax import lax

E = 128
TAB = 16
R = 512
POOL = 8
B_DEV = 128
HOT = 2048
COLD_DEV = 1024
CAP = 16
W = 2176
SAMPLES = 65536
COLD = 65536
N_WIDE = 64
N_GRP = 8


def plan_counts(key):
    key_base, key_load, key_full = jax.random.split(key, 3)
    base_draw = jax.random.randint(key_base, (N_GRP, N_WIDE, N_WIDE), 0, CAP)
    load_draw = jax.random.randint(key_load, (N_GRP, 1, N_WIDE), 2, 5)
    counts = jnp.minimum(1 + base_draw * load_draw // 4, CAP)
    full_owner = jax.random.randint(key_full, (N_GRP, 1, 1), 0, N_WIDE)
    owner_index = jnp.arange(N_WIDE, dtype=jnp.int32)[None, None, :]
    return jnp.where(owner_index == full_owner, CAP, counts).astype(jnp.int32)


def draw_cold_offset(key, part):
    counts = plan_counts(key)
    key = jax.random.fold_in(key, 11)
    values = jax.random.randint(key, (N_GRP, N_WIDE, N_WIDE, CAP), 0, COLD_DEV)
    slot_index = jnp.arange(CAP, dtype=jnp.int32)
    return jnp.where(slot_index < counts[..., None], values, -1).astype(jnp.int32)


def draw_bag_slots(key, part):
    counts = plan_counts(key)
    key = jax.random.fold_in(key, 12)
    key_pick, key_hot, key_peer, key_spin = jax.random.split(key, 4)
    shape = (TAB, SAMPLES, POOL)
    hot_pick = jax.random.randint(key_pick, shape, 0, 2)
    hot_slot = jax.random.randint(key_hot, shape, 0, HOT)
    peer_draw = jax.random.randint(key_peer, shape, 0, N_WIDE)
    spin_draw = jax.random.randint(key_spin, shape, 0, 1048576)
    group_index = (jnp.arange(TAB, dtype=jnp.int32) // (TAB // N_GRP))[:, None, None]
    asker_index = (jnp.arange(SAMPLES, dtype=jnp.int32) // (SAMPLES // N_WIDE))[None, :, None]
    live_count = counts[group_index, asker_index, peer_draw]
    cold_slot = HOT + peer_draw * CAP + spin_draw % live_count
    return jnp.where(hot_pick == 1, hot_slot, cold_slot).astype(jnp.int32)


def plant(entries, key, smallest, top_value):
    index_at = [jax.random.randint(jax.random.fold_in(key, axis), (), 0, length) for axis, length in enumerate(entries.shape)]
    widest = entries.shape.index(max(entries.shape))
    neighbour = index_at[:widest] + [(index_at[widest] + 1) % entries.shape[widest]] + index_at[widest + 1:]
    return entries.at[tuple(index_at)].set(smallest).at[tuple(neighbour)].set(top_value)


def steps_of(stream_key, dims, cuts, smallest, high):
    level = 1.0
    for axis_at, parts in cuts:
        heights = jax.random.uniform(jax.random.fold_in(jax.random.fold_in(stream_key, 6), axis_at), (parts,), jnp.float32, smallest / len(cuts), high / len(cuts))
        level = level * jnp.repeat(jnp.exp(heights), dims[axis_at] // parts).reshape((-1,) + (1,) * (len(dims) - 1 - axis_at))
    return level


def centred(rng, extent, width, limit, pieces=(), kind=jnp.bfloat16):
    values = width * jax.random.normal(rng, extent, jnp.float32)
    if pieces:
        values = values * steps_of(rng, extent, pieces, -0.22, 0.18)
    return jnp.clip(values, -limit, limit).astype(kind)


def setup_inputs(seed: int = 0) -> dict:
    key_list = jax.random.split(jax.random.key(seed), 13)
    return {
        "dense_features": centred(key_list[0], (SAMPLES, E), 1.0, 6.0, ((0, 512),)),
        "bag_slots": draw_bag_slots(jax.random.fold_in(key_list[12], 71), 0),
        "cold_offset": draw_cold_offset(jax.random.fold_in(key_list[12], 71), 0),
        "hot_rows": centred(key_list[3], (N_GRP, HOT, E), 0.35, 2.0, ((0, 8),), jnp.float32),
        "hot_accum": jnp.clip(jnp.exp(math.log(0.01) - 4.6051702 * jax.random.uniform(key_list[4], (N_GRP, HOT), jnp.float32) ** steps_of(key_list[4], (N_GRP, HOT), ((0, 8),), -0.2, 0.2)), 0.0001, 0.01),
        "cold_rows": centred(key_list[5], (N_GRP, COLD, E), 0.35, 2.0, ((0, 8), (1, 64)), jnp.float32),
        "cold_accum": jnp.clip(jnp.exp(math.log(0.01) - 4.6051702 * jax.random.uniform(key_list[6], (N_GRP, COLD), jnp.float32) ** steps_of(key_list[6], (N_GRP, COLD), ((0, 8), (1, 64)), -0.2, 0.2)), 0.0001, 0.01),
        "cross_down": centred(key_list[7], (W, R), W ** -0.5, 0.125, ((0, 64),)),
        "cross_up": centred(key_list[8], (R, W), R ** -0.5, 0.25, ((0, 64),)),
        "cross_bias": centred(key_list[9], (W,), 0.5, 3.0, (), jnp.float32),
        "out_weight": centred(key_list[10], (W,), W ** -0.5, 0.125),
        "labels": plant(jax.random.randint(key_list[11], (SAMPLES,), 0, 2), jax.random.fold_in(key_list[11], 1), 0, 1).astype(jnp.int32),
    }


LEARN = 0.1
EPSILON = 1e-08

def adagrad(table_rows, accumulator, gradient):
    new_accumulator = accumulator + lax.optimization_barrier(jnp.mean(gradient * gradient, axis=-1))
    new_rows = table_rows - LEARN * gradient / (jnp.sqrt(new_accumulator)[..., None] + EPSILON)
    return (new_rows, new_accumulator)

def cross_block(dense_rows, pooled, label_rows, cross_down, cross_up, cross_bias, out_weight):
    sample_count = dense_rows.shape[0]
    stacked = jnp.concatenate([dense_rows, jnp.transpose(pooled, (1, 0, 2)).reshape(sample_count, TAB * E)], axis=1)
    low_rank = jnp.dot(stacked, cross_down, preferred_element_type=jnp.float32).astype(jnp.bfloat16)
    cross_gain = jnp.dot(low_rank, cross_up, preferred_element_type=jnp.float32) + cross_bias
    stacked_wide = stacked.astype(jnp.float32)
    crossed = stacked_wide * cross_gain + stacked_wide
    head_weight = out_weight.astype(jnp.float32)
    logits = lax.optimization_barrier(jnp.sum(crossed * head_weight, axis=1))
    residual_grad = jax.nn.sigmoid(logits) - label_rows.astype(jnp.float32)
    d_crossed = residual_grad[:, None] * head_weight
    d_gain = (d_crossed * stacked_wide).astype(jnp.bfloat16)
    d_low = lax.dot_general(d_gain, cross_up, (((1,), (1,)), ((), ())), preferred_element_type=jnp.float32).astype(jnp.bfloat16)
    d_stacked = d_crossed * (cross_gain + 1.0) + lax.dot_general(d_low, cross_down, (((1,), (1,)), ((), ())), preferred_element_type=jnp.float32)
    d_pooled = jnp.transpose(d_stacked[:, E:].reshape(sample_count, TAB, E), (1, 0, 2)).astype(jnp.bfloat16)
    return (logits, d_pooled)

def reference(dense_features, bag_slots, cold_offset, hot_rows, hot_accum, cold_rows, cold_accum, cross_down, cross_up, cross_bias, out_weight, labels):
    block_size = B_DEV * N_GRP
    per_group = TAB // N_GRP
    slot_total = HOT + N_WIDE * CAP
    hot_bf = hot_rows.astype(jnp.bfloat16)
    cold_bf = cold_rows.astype(jnp.bfloat16)
    group_of = (jnp.arange(TAB, dtype=jnp.int32) // per_group).astype(jnp.int32)
    owners = (jnp.arange(N_WIDE, dtype=jnp.int32) * COLD_DEV)[None, :, None]
    group_base = (jnp.arange(N_GRP, dtype=jnp.int32) * COLD)[:, None, None]

    def block_step(totals, wide_index):
        hot_grad, cold_grad = totals
        first_row = (wide_index * block_size).astype(jnp.int32)
        slot_ids = lax.dynamic_slice_in_dim(bag_slots, first_row, block_size, 1)
        asked_rows = lax.dynamic_index_in_dim(cold_offset, wide_index, 1, keepdims=False)
        live_slot = asked_rows >= 0
        where_rows = (owners + jnp.maximum(asked_rows, 0)).astype(jnp.int32)
        fetched = jax.vmap(lambda source, chosen: source[chosen])(cold_bf, where_rows.reshape(N_GRP, -1))
        fetched = jnp.where(live_slot.reshape(N_GRP, -1, 1), fetched, jnp.zeros((), jnp.bfloat16))
        buffer = jnp.concatenate([hot_bf, fetched], axis=1)
        table_buffer = buffer[group_of]
        picked = jax.vmap(lambda source, chosen: source[chosen])(table_buffer, slot_ids)
        pooled = lax.optimization_barrier(jnp.sum(picked.astype(jnp.float32), axis=2)).astype(jnp.bfloat16)
        dense_rows = lax.dynamic_slice_in_dim(dense_features, first_row, block_size, 0)
        label_rows = lax.dynamic_slice_in_dim(labels, first_row, block_size, 0)
        logits, d_pooled = cross_block(dense_rows, pooled, label_rows, cross_down, cross_up, cross_bias, out_weight)
        spread = jnp.broadcast_to(d_pooled.astype(jnp.float32)[:, :, None, :], (TAB, block_size, POOL, E))
        flat_slots = (group_of[:, None, None] * slot_total + slot_ids).astype(jnp.int32).reshape(-1)
        slot_grad = jnp.zeros((N_GRP * slot_total, E), jnp.float32).at[flat_slots].add(spread.reshape(-1, E))
        slot_grad = slot_grad.reshape(N_GRP, slot_total, E)
        hot_grad = hot_grad + slot_grad[:, :HOT]
        cold_part = slot_grad[:, HOT:]
        target = jnp.where(live_slot, group_base + where_rows, N_GRP * COLD).astype(jnp.int32)
        cold_grad = cold_grad.at[target.reshape(-1)].add(cold_part.reshape(-1, E), mode='drop')
        return ((hot_grad, cold_grad), logits)
    initial = (jnp.zeros((N_GRP, HOT, E), jnp.float32), jnp.zeros((N_GRP * COLD, E), jnp.float32))
    (hot_grad, cold_grad), logits = lax.scan(block_step, initial, jnp.arange(N_WIDE, dtype=jnp.int32))
    new_hot_rows, new_hot_accum = adagrad(hot_rows, hot_accum, hot_grad)
    new_cold_rows, new_cold_accum = adagrad(cold_rows, cold_accum, cold_grad.reshape(N_GRP, COLD, E))
    return (logits.reshape(SAMPLES), new_hot_rows, new_hot_accum, new_cold_rows, new_cold_accum)
```

```python
import functools

import jax
import jax.numpy as jnp
from jax import lax
from jax.experimental import pallas as pl
from jax.experimental.pallas import tpu as pltpu
from jax.sharding import PartitionSpec as P

LEARN = 0.1
EPSILON = 1e-08
LANES = 128
BF = jnp.bfloat16
F32 = jnp.float32


def wide_shape(n_wide):
    return {64: (4, 8, 2), 8: (2, 2, 2)}[n_wide]


def greet(axis, count, me):
    barrier = pltpu.get_barrier_semaphore()

    def hello(step, carry):
        pl.semaphore_signal(
            barrier, inc=1, device_id={axis: lax.rem(me + step, count)}, device_id_type=pl.DeviceIdType.MESH
        )
        return carry

    lax.fori_loop(1, count, hello, 0)
    pl.semaphore_wait(barrier, count - 1)


def push(src, dst, send_sem, recv_sem, target):
    return pltpu.make_async_remote_copy(
        src_ref=src,
        dst_ref=dst,
        send_sem=send_sem,
        recv_sem=recv_sem,
        device_id=target,
        device_id_type=pl.DeviceIdType.MESH,
    )


def fetch_kernel(
    n_wide, ask_ref, cold_ref, shard_ref,
    fetched_ref, asked_out, gathered_ref,
    asked, cold_bf, picked, columns,
    ask_send, ask_recv, row_send, row_recv, x_send, x_recv, up_send, up_recv, dn_send, dn_recv, sib_send, sib_recv, own_sem,
):
    nx, ny, nc = wide_shape(n_wide)
    me = lax.axis_index("wide")
    core = lax.rem(me, nc)
    y = lax.rem(me // nc, ny)
    x = me // (nc * ny)
    sibling = {"wide": me + 1 - 2 * core}
    greet("wide", n_wide, me)

    def at_wide(x_, y_, c_):
        return {"wide": (x_ * ny + y_) * nc + c_}

    def ask_copy(other):
        return push(ask_ref.at[other], asked.at[me], ask_send.at[other], ask_recv.at[me], {"wide": other})

    def ask_from(other):
        return push(ask_ref.at[me], asked.at[other], ask_send.at[me], ask_recv.at[other], {"wide": other})

    def ask_step(step, carry):
        ask_copy(lax.rem(me + step, n_wide)).start()
        return carry

    lax.fori_loop(1, n_wide, ask_step, 0)
    asked[me] = ask_ref[me]

    own = pltpu.make_async_copy(shard_ref, gathered_ref.at[y, core, x], own_sem)
    own.start()
    x_copies = []
    for step in range(1, nx):
        copy = push(
            shard_ref, gathered_ref.at[y, core, x], x_send.at[step], x_recv.at[step],
            at_wide(lax.rem(x + step, nx), y, core),
        )
        copy.start()
        x_copies.append(copy)

    cold_bf[...] = cold_ref[...].astype(BF)

    own.wait()
    for copy in x_copies:
        copy.wait()
    above, below = lax.rem(y + 1, ny), lax.rem(y + ny - 1, ny)
    n_up, n_dn = ny // 2, (ny - 1) // 2

    def block(row):
        return gathered_ref.at[row, core]

    def up_copy(step):
        row = lax.rem(y + ny - step, ny)
        return push(block(row), block(row), up_send.at[step], up_recv.at[step], at_wide(x, above, core))

    def dn_copy(step):
        row = lax.rem(y + step, ny)
        return push(block(row), block(row), dn_send.at[step], dn_recv.at[step], at_wide(x, below, core))

    def sib_copy(index, row):
        return push(block(row), block(row), sib_send.at[index], sib_recv.at[index], sibling)

    up_copy(0).start()
    if n_dn:
        dn_copy(0).start()
    sib_copy(0, y).start()

    def ask_wait(step, carry):
        ask_from(lax.rem(me + step, n_wide)).wait_recv()
        return carry

    lax.fori_loop(1, n_wide, ask_wait, 0)
    cap = picked.shape[1]
    owned = cold_bf.shape[0]
    per_batch = LANES // cap

    def batch_step(batch, carry):
        spread = jnp.concatenate(
            [jnp.broadcast_to(asked[batch * per_batch + k], (cap, LANES)) for k in range(per_batch)], axis=0
        ).astype(F32)
        lane = lax.broadcasted_iota(jnp.int32, (LANES, LANES), 1)
        row = lax.broadcasted_iota(jnp.int32, (LANES, LANES), 0)
        kept = jnp.where(lane == lax.rem(row, cap), spread, 0.0)
        column = jnp.sum(kept, axis=1, keepdims=True)
        asked_out[pl.ds(batch, 1), :] = jnp.sum(
            jnp.transpose(kept), axis=0, keepdims=True
        ).astype(jnp.int32)
        wanted = column.astype(jnp.int32)
        columns_iota = lax.broadcasted_iota(jnp.int32, (LANES, owned), 1)
        chosen = jnp.where(columns_iota == wanted, 1.0, 0.0).astype(BF)
        rows = jnp.dot(chosen, cold_bf[...], preferred_element_type=F32).astype(BF)
        for k in range(per_batch):
            picked[batch * per_batch + k] = rows[k * cap : (k + 1) * cap]
        return carry

    lax.fori_loop(0, n_wide // per_batch, batch_step, 0)

    def row_copy(other):
        return push(picked.at[other], fetched_ref.at[me], row_send.at[other], row_recv.at[me], {"wide": other})

    def row_from(other):
        return push(picked.at[me], fetched_ref.at[other], row_send.at[me], row_recv.at[other], {"wide": other})

    def row_step(step, carry):
        row_copy(lax.rem(me + step, n_wide)).start()
        return carry

    lax.fori_loop(1, n_wide, row_step, 0)
    fetched_ref[me] = picked[me]

    for step in range(n_up):
        up_copy(step).wait_recv()
        if step + 1 < n_up:
            up_copy(step + 1).start()
        sib_copy(1 + step, lax.rem(y + ny - step - 1, ny)).start()
        if step < n_dn:
            dn_copy(step).wait_recv()
            if step + 1 < n_dn:
                dn_copy(step + 1).start()
            sib_copy(1 + n_up + step, lax.rem(y + step + 1, ny)).start()
    for step in range(n_up):
        up_copy(step).wait_send()
    for step in range(n_dn):
        dn_copy(step).wait_send()
    for index in range(ny):
        sib_copy(index, y).wait()

    def finish(step, carry):
        other = lax.rem(me + step, n_wide)
        ask_copy(other).wait_send()
        row_copy(other).wait_send()
        row_from(other).wait_recv()
        return carry

    lax.fori_loop(1, n_wide, finish, 0)


def cross_kernel(
    n_grp, slots_ref, hot_ref, fetched_ref, dense_ref, down_ref, up_ref, bias_ref, head_ref, labels_ref,
    logits_ref, hot_out, cold_out,
    buffer_t, counts, pooled_out, stacked, gain, d_low, d_out, d_in, slot_grad,
    p_send, p_recv, d_send, d_recv,
):
    me = lax.axis_index("grp")
    hot_count, width = hot_ref.shape
    slot_total = buffer_t.shape[1]
    samples = dense_ref.shape[0]
    his = slot_total // LANES
    words = -(-his // 8)
    pool = slots_ref.shape[1]
    greet("grp", n_grp, me)

    stacked[:, :width] = dense_ref[...]
    for k in range(hot_count // LANES):
        rows = pl.ds(k * LANES, LANES)
        buffer_t[:, k * LANES : (k + 1) * LANES] = jnp.transpose(hot_ref[rows, :]).astype(BF)
    for k in range((slot_total - hot_count) // LANES):
        part = fetched_ref[k * LANES : (k + 1) * LANES, :].astype(F32)
        at = hot_count + k * LANES
        buffer_t[:, at : at + LANES] = jnp.transpose(part).astype(BF)

    def pooled_copy(other):
        return push(
            pooled_out.at[other],
            stacked.at[:, pl.ds(pl.multiple_of(width + 2 * width * me, LANES), 2 * width)],
            p_send.at[other], p_recv.at[me], {"grp": other},
        )

    def pooled_from(other):
        return push(
            pooled_out.at[me],
            stacked.at[:, pl.ds(pl.multiple_of(width + 2 * width * other, LANES), 2 * width)],
            p_send.at[me], p_recv.at[other], {"grp": other},
        )

    def count_chunk(chunk):
        at = pl.ds(pl.multiple_of(chunk * samples, LANES), samples)
        slots = jnp.concatenate([slots_ref[0, :, at], slots_ref[1, :, at]], axis=1)
        low = lax.bitwise_and(slots, LANES - 1)
        high = lax.shift_right_logical(slots, 7)
        unit = lax.shift_left(jnp.ones_like(high), 4 * lax.bitwise_and(high, 7))
        parts = [jnp.where(lax.shift_right_logical(high, 3) == k, unit, 0) for k in range(words)]

        def rows_step(q, carry):
            ids = lax.broadcasted_iota(jnp.int32, (16, 2 * samples), 0) + q * 16
            total = [jnp.zeros((16, 2 * samples), jnp.int32) for _ in range(words)]
            for l in range(pool):
                hit = ids == low[l : l + 1, :]
                for k in range(words):
                    total[k] = total[k] + jnp.where(hit, parts[k][l : l + 1, :], 0)
            for h in range(his):
                digit = lax.bitwise_and(lax.shift_right_logical(total[h // 8], 4 * (h % 8)), 15)
                counts[chunk, pl.ds(pl.multiple_of(h * LANES + q * 16, 16), 16), :] = digit.astype(F32).astype(BF)
            return carry

        lax.fori_loop(0, LANES // 16, rows_step, 0)

    def pool_step(step, carry):
        chunk = lax.rem(me + jnp.where(step == n_grp - 1, 0, step + 1), n_grp)
        count_chunk(chunk)
        pooled_t = jnp.dot(buffer_t[...], counts[chunk], preferred_element_type=F32)
        for t in range(2):
            pooled_out[chunk, :, t * width : (t + 1) * width] = jnp.transpose(
                pooled_t[:, t * samples : (t + 1) * samples]
            ).astype(BF)

        @pl.when(step < n_grp - 1)
        def _():
            pooled_copy(chunk).start()

        return carry

    lax.fori_loop(0, n_grp, pool_step, 0)
    stacked[:, pl.ds(pl.multiple_of(width + 2 * width * me, LANES), 2 * width)] = pooled_out[me]

    def pooled_wait(step, carry):
        other = lax.rem(me + step, n_grp)
        pooled_copy(other).wait_send()
        pooled_from(other).wait_recv()
        return carry

    lax.fori_loop(1, n_grp, pooled_wait, 0)

    low_rank = jnp.dot(stacked[...], down_ref[...], preferred_element_type=F32).astype(BF)
    columns = stacked.shape[1]
    partial = jnp.zeros((samples, LANES), F32)
    for k in range(columns // LANES):
        at = slice(k * LANES, (k + 1) * LANES)
        wide = stacked[:, at].astype(F32)
        part = jnp.dot(low_rank, up_ref[:, at], preferred_element_type=F32) + bias_ref[:, at]
        gain[:, at] = part
        partial = partial + (wide * part + wide) * head_ref[:, at].astype(F32)
    logits = jnp.sum(jnp.transpose(partial), axis=0, keepdims=True)
    logits_ref[...] = logits
    residual = jax.nn.sigmoid(logits) - labels_ref[...].astype(F32)
    residual = jnp.transpose(jnp.broadcast_to(residual, (LANES, samples)))
    low_grad = jnp.zeros((samples, low_rank.shape[1]), F32)
    for k in range(columns // LANES):
        at = slice(k * LANES, (k + 1) * LANES)
        d_crossed = residual * head_ref[:, at].astype(F32)
        d_gain = (d_crossed * stacked[:, at].astype(F32)).astype(BF)
        low_grad = low_grad + lax.dot_general(
            d_gain, up_ref[:, at], (((1,), (1,)), ((), ())), preferred_element_type=F32
        )
    d_low[...] = low_grad.astype(BF)

    def d_copy(other):
        return push(d_out.at[other], d_in.at[me], d_send.at[other], d_recv.at[me], {"grp": other})

    def d_from(other):
        return push(d_out.at[me], d_in.at[other], d_send.at[me], d_recv.at[other], {"grp": other})

    def back_step(step, carry):
        other = lax.rem(me + jnp.where(step == n_grp - 1, 0, step + 1), n_grp)
        at = pl.ds(pl.multiple_of(width + 2 * width * other, LANES), 2 * width)
        back = lax.dot_general(
            d_low[...], down_ref[at, :], (((1,), (1,)), ((), ())), preferred_element_type=F32
        )
        d_crossed = jnp.concatenate([residual, residual], axis=1) * head_ref[:, at].astype(F32)
        d_out[other] = (d_crossed * (gain[:, at] + 1.0) + back).astype(BF)

        @pl.when(step < n_grp - 1)
        def _():
            d_copy(other).start()

        return carry

    lax.fori_loop(0, n_grp, back_step, 0)
    d_in[me] = d_out[me]

    def grad_chunk(chunk, first):
        both = d_in[chunk]
        d_rows = jnp.concatenate([both[:, :width], both[:, width:]], axis=0)
        tile = 4 * LANES if slot_total % (4 * LANES) == 0 else LANES

        def tile_step(i, carry):
            at = pl.ds(pl.multiple_of(i * tile, tile), tile)
            part = jnp.dot(counts[chunk, at, :], d_rows, preferred_element_type=F32)
            slot_grad[at, :] = part if first else slot_grad[at, :] + part
            return carry

        lax.fori_loop(0, slot_total // tile, tile_step, 0)

    grad_chunk(me, True)

    def grad_step(step, carry):
        other = lax.rem(me + n_grp - step, n_grp)
        d_copy(other).wait_send()
        d_from(other).wait_recv()
        grad_chunk(other, False)
        return carry

    lax.fori_loop(1, n_grp, grad_step, 0)
    hot_out[...] = slot_grad[:hot_count, :].astype(BF)
    cold_out[...] = slot_grad[hot_count:, :].astype(BF).reshape(cold_out.shape)


def adagrad_rows(rows_ref, accum_ref, gradient, new_rows_ref, new_accum_ref, at):
    square = jnp.sum(jnp.transpose(gradient * gradient), axis=0, keepdims=True)
    accum = accum_ref[:, at] + square / LANES
    new_accum_ref[:, at] = accum
    scale = jnp.transpose(jnp.broadcast_to(jnp.sqrt(accum) + EPSILON, (LANES, LANES)))
    new_rows_ref[at, :] = rows_ref[at, :] - LEARN * gradient / scale


def update_kernel(
    n_wide, hot_grad, cold_grad, asked_ref, hot_ref, hot_accum, cold_ref, cold_accum,
    new_hot, new_hot_accum, new_cold, new_cold_accum,
    cold_in, pair_in, half, rs_in, total, chosen, cold_sum,
    c_send, c_recv, pair_send, pair_recv, rs_send, rs_recv, ag_send, ag_recv, sib_send, sib_recv,
):
    nx, ny, nc = wide_shape(n_wide)
    chips = nx * ny
    me = lax.axis_index("wide")
    core = lax.rem(me, nc)
    chip = me // nc
    sibling = {"wide": me + 1 - 2 * core}
    hot_count = hot_ref.shape[0]
    per_half = hot_count // 2
    per_chip = per_half // chips
    owned = cold_ref.shape[0]
    greet("wide", n_wide, me)

    def half_at(c):
        return pl.ds(pl.multiple_of(c * per_half, per_half), per_half)

    def chip_at(q):
        return pl.ds(pl.multiple_of(q * per_chip, per_chip), per_chip)

    pair = push(hot_grad.at[half_at(1 - core)], pair_in, pair_send, pair_recv, sibling)
    pair.start()

    def cold_copy(other):
        return push(cold_grad.at[other], cold_in.at[me], c_send.at[other], c_recv.at[me], {"wide": other})

    def cold_from(other):
        return push(cold_grad.at[me], cold_in.at[other], c_send.at[me], c_recv.at[other], {"wide": other})

    def cold_step(step, carry):
        cold_copy(lax.rem(me + step, n_wide)).start()
        return carry

    lax.fori_loop(1, n_wide, cold_step, 0)
    cold_in[me] = cold_grad[me]

    pair.wait()
    half[...] = (hot_grad[half_at(core), :].astype(F32) + pair_in[...].astype(F32)).astype(BF)

    def rs_copy(q):
        return push(
            half.at[chip_at(q)], rs_in.at[chip], rs_send.at[q], rs_recv.at[chip], {"wide": q * nc + core}
        )

    def rs_from(q):
        return push(
            half.at[chip_at(q)], rs_in.at[q], rs_send.at[q], rs_recv.at[q], {"wide": q * nc + core}
        )

    def rs_step(step, carry):
        rs_copy(lax.rem(chip + step, chips)).start()
        return carry

    lax.fori_loop(1, chips, rs_step, 0)
    rs_in[chip] = half[chip_at(chip), :]

    def fill(batch, carry):
        ids = lax.broadcasted_iota(jnp.int32, (owned, LANES), 0)
        chosen[:, pl.ds(pl.multiple_of(batch * LANES, LANES), LANES)] = jnp.where(
            ids == asked_ref[pl.ds(batch, 1), :], 1.0, 0.0
        ).astype(BF)
        return carry

    lax.fori_loop(0, chosen.shape[1] // LANES, fill, 0)

    def cold_wait(step, carry):
        other = lax.rem(me + step, n_wide)
        cold_from(other).wait_recv()
        cold_copy(other).wait_send()
        return carry

    lax.fori_loop(1, n_wide, cold_wait, 0)
    arrived = cold_in[...].reshape(chosen.shape[1], LANES)
    cold_sum[...] = jnp.dot(chosen[...], arrived, preferred_element_type=F32)

    def cold_update(i, carry):
        at = pl.ds(pl.multiple_of(i * LANES, LANES), LANES)
        adagrad_rows(cold_ref, cold_accum, cold_sum[at, :], new_cold, new_cold_accum, at)
        return carry

    lax.fori_loop(0, owned // LANES, cold_update, 0)

    def rs_wait(step, carry):
        q = lax.rem(chip + step, chips)
        rs_from(q).wait_recv()
        rs_copy(q).wait_send()
        return carry

    lax.fori_loop(1, chips, rs_wait, 0)

    def own_at(c, q):
        return pl.ds(pl.multiple_of(c * per_half + q * per_chip, per_chip), per_chip)

    def add(q, so_far):
        return so_far + rs_in[q].astype(F32)

    summed = lax.fori_loop(0, chips, add, jnp.zeros((per_chip, LANES), F32))
    total[own_at(core, chip), :] = summed.astype(BF)

    def ag_copy(q):
        return push(
            total.at[own_at(core, chip)], total.at[own_at(core, chip)], ag_send.at[q], ag_recv.at[chip],
            {"wide": q * nc + core},
        )

    def ag_from(q):
        return push(
            total.at[own_at(core, q)], total.at[own_at(core, q)], ag_send.at[q], ag_recv.at[q],
            {"wide": q * nc + core},
        )

    def ag_step(step, carry):
        ag_copy(lax.rem(chip + step, chips)).start()
        return carry

    lax.fori_loop(1, chips, ag_step, 0)

    def ag_wait(step, carry):
        q = lax.rem(chip + step, chips)
        ag_from(q).wait_recv()
        ag_copy(q).wait_send()
        return carry

    lax.fori_loop(1, chips, ag_wait, 0)
    sib = push(total.at[half_at(core)], total.at[half_at(core)], sib_send, sib_recv, sibling)
    sib.start()

    def hot_update(c):
        def step(i, carry):
            at = pl.ds(pl.multiple_of(c * per_half + i * LANES, LANES), LANES)
            adagrad_rows(hot_ref, hot_accum, total[at, :].astype(F32), new_hot, new_hot_accum, at)
            return carry

        lax.fori_loop(0, per_half // LANES, step, 0)

    hot_update(core)
    sib.wait()
    hot_update(1 - core)


VMEM = pl.BlockSpec(memory_space=pltpu.VMEM)
ANY = pl.BlockSpec(memory_space=pl.ANY)
DMA = pltpu.SemaphoreType.DMA


def params(collective_id):
    return pltpu.CompilerParams(
        collective_id=collective_id, has_side_effects=True, vmem_limit_bytes=56 * 1024 * 1024
    )


def on_device(
    n_wide, n_grp,
    dense_features, bag_slots, cold_offset, hot_rows, hot_accum, cold_rows, cold_accum,
    cross_down, cross_up, cross_bias, out_weight, labels,
):
    nx, ny, nc = wide_shape(n_wide)
    samples, width = dense_features.shape
    hot_count = hot_rows.shape[1]
    owned = cold_rows.shape[1]
    cap = cold_offset.shape[3]
    requests = n_wide * cap
    slot_total = hot_count + requests
    down_rows, rank = cross_down.shape
    up_rows, columns = cross_up.shape
    down_size, up_size = (down_rows * rank // LANES, up_rows * columns // LANES)
    shard = jnp.concatenate(
        [
            cross_down.reshape(down_rows, rank // LANES, LANES).transpose(1, 0, 2).reshape(down_size, LANES),
            cross_up.reshape(up_rows, columns // LANES, LANES).transpose(1, 0, 2).reshape(up_size, LANES),
        ]
    )
    ask = jnp.pad(cold_offset[0, 0], ((0, 0), (0, LANES - cap))).reshape(n_wide, 1, LANES)
    fetched, asked, gathered = pl.pallas_call(
        functools.partial(fetch_kernel, n_wide),
        out_shape=(
            jax.ShapeDtypeStruct((n_wide, cap, width), BF),
            jax.ShapeDtypeStruct((requests // LANES, LANES), jnp.int32),
            jax.ShapeDtypeStruct((ny, nc, nx) + shard.shape, BF),
        ),
        in_specs=[VMEM, VMEM, ANY],
        out_specs=(VMEM, VMEM, ANY),
        scratch_shapes=[
            pltpu.VMEM((n_wide, 1, LANES), jnp.int32),
            pltpu.VMEM((owned, width), BF),
            pltpu.VMEM((n_wide, cap, width), BF),
            pltpu.VMEM((LANES, LANES), F32),
            DMA((n_wide,)), DMA((n_wide,)), DMA((n_wide,)), DMA((n_wide,)),
            DMA((nx,)), DMA((nx,)), DMA((ny,)), DMA((ny,)), DMA((ny,)), DMA((ny,)), DMA((ny,)), DMA((ny,)),
            DMA,
        ],
        compiler_params=params(0),
        name="fetch_and_gather",
    )(ask, cold_rows[0], shard)

    ordered = gathered.transpose(2, 0, 1, 3, 4).reshape(n_wide, down_size + up_size, LANES)
    down_full = (
        ordered[:, :down_size].reshape(n_wide, rank // LANES, down_rows, LANES)
        .transpose(0, 2, 1, 3).reshape(n_wide * down_rows, rank)
    )
    up_full = (
        ordered[:, down_size:].reshape(n_wide, columns // LANES, up_rows, LANES)
        .transpose(0, 2, 1, 3).reshape(n_wide * up_rows, columns)
    )

    slots = jnp.transpose(bag_slots, (0, 2, 1))
    logits, hot_grad, cold_grad = pl.pallas_call(
        functools.partial(cross_kernel, n_grp),
        out_shape=(
            jax.ShapeDtypeStruct((1, samples), F32),
            jax.ShapeDtypeStruct((hot_count, width), BF),
            jax.ShapeDtypeStruct((n_wide, cap, width), BF),
        ),
        in_specs=[VMEM] * 9,
        out_specs=(VMEM, VMEM, VMEM),
        scratch_shapes=[
            pltpu.VMEM((width, slot_total), BF),
            pltpu.VMEM((n_grp, slot_total, 2 * samples), BF),
            pltpu.VMEM((n_grp, samples, 2 * width), BF),
            pltpu.VMEM((samples, columns), BF),
            pltpu.VMEM((samples, columns), F32),
            pltpu.VMEM((samples, rank), BF),
            pltpu.VMEM((n_grp, samples, 2 * width), BF),
            pltpu.VMEM((n_grp, samples, 2 * width), BF),
            pltpu.VMEM((slot_total, width), F32),
            DMA((n_grp,)), DMA((n_grp,)), DMA((n_grp,)), DMA((n_grp,)),
        ],
        compiler_params=params(1),
        name="pool_cross_grad",
    )(
        slots, hot_rows[0], fetched.reshape(requests, width), dense_features, down_full, up_full,
        cross_bias.reshape(1, columns), out_weight.reshape(1, columns), labels.reshape(1, samples),
    )

    chips = nx * ny
    per_chip = hot_count // 2 // chips
    new_hot, new_hot_accum, new_cold, new_cold_accum = pl.pallas_call(
        functools.partial(update_kernel, n_wide),
        out_shape=(
            jax.ShapeDtypeStruct((hot_count, width), F32),
            jax.ShapeDtypeStruct((1, hot_count), F32),
            jax.ShapeDtypeStruct((owned, width), F32),
            jax.ShapeDtypeStruct((1, owned), F32),
        ),
        in_specs=[VMEM] * 7,
        out_specs=(VMEM,) * 4,
        scratch_shapes=[
            pltpu.VMEM((n_wide, cap, width), BF),
            pltpu.VMEM((hot_count // 2, width), BF),
            pltpu.VMEM((hot_count // 2, width), BF),
            pltpu.VMEM((chips, per_chip, width), BF),
            pltpu.VMEM((hot_count, width), BF),
            pltpu.VMEM((owned, requests), BF),
            pltpu.VMEM((owned, width), F32),
            DMA((n_wide,)), DMA((n_wide,)), DMA, DMA,
            DMA((chips,)), DMA((chips,)), DMA((chips,)), DMA((chips,)), DMA, DMA,
        ],
        compiler_params=params(2),
        name="exchange_and_update",
    )(hot_grad, cold_grad, asked, hot_rows[0], hot_accum, cold_rows[0], cold_accum)
    return (logits.reshape(samples), new_hot[None], new_hot_accum, new_cold[None], new_cold_accum)


def solution(mesh):
    return jax.shard_map(
        functools.partial(on_device, mesh.shape["wide"], mesh.shape["grp"]),
        mesh=mesh,
        in_specs=(
            P(("wide", "grp"), None),
            P("grp", "wide", None),
            P("grp", "wide", None, None),
            P("grp", None, None),
            P("grp", None),
            P("grp", "wide", None),
            P("grp", "wide"),
            P("wide", None),
            P("wide", None),
            P(),
            P(),
            P(("wide", "grp")),
        ),
        out_specs=(
            P(("wide", "grp")),
            P("grp", None, None),
            P("grp", None),
            P("grp", "wide", None),
            P("grp", "wide"),
        ),
        check_vma=False,
    )
```

```python
import functools

import jax
import jax.numpy as jnp
from jax import lax
from jax.experimental import pallas as pl
from jax.experimental.pallas import tpu as pltpu
from jax.sharding import PartitionSpec as P

LEARN = 0.1
EPSILON = 1e-08
LANES = 128
BF = jnp.bfloat16
F32 = jnp.float32


def wide_shape(n_wide):
    return {64: (4, 8, 2), 8: (2, 2, 2)}[n_wide]


def round_up(value, unit):
    return -(-value // unit) * unit


def push(src, dst, send_sem, recv_sem, target):
    return pltpu.make_async_remote_copy(
        src_ref=src,
        dst_ref=dst,
        send_sem=send_sem,
        recv_sem=recv_sem,
        device_id=target,
        device_id_type=pl.DeviceIdType.MESH,
    )


def each(first, last, body):
    def step(i, carry):
        body(i)
        return carry

    lax.fori_loop(first, last, step, 0)


def far_first(count):
    return sorted(range(1, count), key=lambda o: -min(o, count - o)) + [0]


def step_kernel(
    n_wide, n_grp,
    offset_ref, cold_ref, down_ref, up_ref, slots_ref, hot_ref, dense_ref, small_ref,
    logits_ref, total_ref, cold_sum_ref,
    ask, asked, asked_lane, cold_bf, picked, fetched,
    shard32, shard_down, shard_up, all_down, all_up, down32, down, up,
    buffer_t, counts, pooled_hot, pooled_out, stacked, gain, d_low, d_out, d_in, slot_grad,
    hot_grad, cold_grad, cold_in, pair_in, half, rs_in, chosen,
    ask_send, ask_recv, row_send, row_recv,
    d1_send, d1_recv, d_up_send, d_up_recv, d_dn_send, d_dn_recv, d_sib_send, d_sib_recv,
    u1_send, u1_recv, u_up_send, u_up_recv, u_dn_send, u_dn_recv, u_sib_send, u_sib_recv,
    p_send, p_recv, g_send, g_recv,
    c_send, c_recv, pair_send, pair_recv, rs_send, rs_recv, ag_send, ag_recv, sib_send, sib_recv,
):
    nx, ny, nc = wide_shape(n_wide)
    chips = nx * ny
    me = lax.axis_index("wide")
    grp = lax.axis_index("grp")
    core = lax.rem(me, nc)
    chip = me // nc
    y = lax.rem(chip, ny)
    x = chip // ny
    sibling = {"wide": me + 1 - 2 * core}
    hot_count, width = hot_ref.shape
    owned = cold_ref.shape[0]
    cap = picked.shape[1]
    slot_total = buffer_t.shape[1]
    samples = dense_ref.shape[0]
    columns = stacked.shape[1]
    his = slot_total // LANES
    words = -(-his // 8)
    pool = slots_ref.shape[1]
    order = far_first(n_grp)

    def at_wide(x_, y_):
        return {"wide": (x_ * ny + y_) * nc + core}

    barrier = pltpu.get_barrier_semaphore()
    for axis, count, mine in (("wide", n_wide, me), ("grp", n_grp, grp)):
        each(1, count, lambda step: pl.semaphore_signal(
            barrier, inc=1, device_id={axis: lax.rem(mine + step, count)}, device_id_type=pl.DeviceIdType.MESH
        ))

    ask[...] = jnp.zeros_like(ask)
    for other in range(n_wide):
        ask[other, :, :cap] = offset_ref[other : other + 1, :]
    down_rows, rank = down_ref.shape
    up_rows = up_ref.shape[0]
    shard32[...] = jnp.zeros_like(shard32)
    for j in range(rank // LANES):
        shard32[j * down_rows : (j + 1) * down_rows, :] = down_ref[:, j * LANES : (j + 1) * LANES].astype(F32)
    shard_down[...] = shard32[...].astype(BF)
    for j in range(columns // LANES):
        shard32[j * up_rows : (j + 1) * up_rows, :] = up_ref[:, j * LANES : (j + 1) * LANES].astype(F32)
    shard_up[...] = shard32[...].astype(BF)
    all_down[y, core, x] = shard_down[...]
    all_up[x, core, y] = shard_up[...]
    pl.semaphore_wait(barrier, n_wide + n_grp - 2)

    def ask_copy(other):
        return push(ask.at[other], asked.at[me], ask_send.at[other], ask_recv.at[me], {"wide": other})

    def ask_from(other):
        return push(ask.at[me], asked.at[other], ask_send.at[me], ask_recv.at[other], {"wide": other})

    each(1, n_wide, lambda step: ask_copy(lax.rem(me + step, n_wide)).start())
    asked[me] = ask[me]

    def down_first(step):
        return push(
            shard_down, all_down.at[y, core, x], d1_send.at[step], d1_recv.at[step], at_wide(lax.rem(x + step, nx), y)
        )

    def up_first(step):
        return push(
            shard_up, all_up.at[x, core, y], u1_send.at[step], u1_recv.at[step], at_wide(x, lax.rem(y + step, ny))
        )

    for step in far_first(nx)[:-1]:
        down_first(step).start()
    for step in far_first(ny)[:-1]:
        up_first(step).start()

    def ring(blocks, mine, length, place, sems):
        fwd_send, fwd_recv, bwd_send, bwd_recv, side_send, side_recv = sems
        n_fwd, n_bwd = length // 2, (length - 1) // 2

        def block(index):
            return blocks.at[index, core]

        def fwd(step):
            held = block(lax.rem(mine + length - step, length))
            return push(held, held, fwd_send.at[step], fwd_recv.at[step], place(lax.rem(mine + 1, length)))

        def bwd(step):
            held = block(lax.rem(mine + step, length))
            return push(held, held, bwd_send.at[step], bwd_recv.at[step], place(lax.rem(mine + length - 1, length)))

        def side(step):
            held = block(lax.rem(mine + length - step, length))
            return push(held, held, side_send.at[step], side_recv.at[step], sibling)

        def start():
            fwd(0).start()
            if n_bwd:
                bwd(0).start()
            side(0).start()

        def serve(step):
            fwd(step).wait_recv()
            if step + 1 < n_fwd:
                fwd(step + 1).start()
            side(step + 1).start()
            if step < n_bwd:
                bwd(step).wait_recv()
                if step + 1 < n_bwd:
                    bwd(step + 1).start()
                side(length - step - 1).start()

        def drain():
            for step in range(n_fwd):
                fwd(step).wait_send()
            for step in range(n_bwd):
                bwd(step).wait_send()
            for step in range(length):
                side(step).wait()

        return start, [functools.partial(serve, step) for step in range(n_fwd)], drain

    down_start, down_serve, down_drain = ring(
        all_down, y, ny, lambda row: at_wide(x, row),
        (d_up_send, d_up_recv, d_dn_send, d_dn_recv, d_sib_send, d_sib_recv),
    )
    up_start, up_serve, up_drain = ring(
        all_up, x, nx, lambda row: at_wide(row, y),
        (u_up_send, u_up_recv, u_dn_send, u_dn_recv, u_sib_send, u_sib_recv),
    )

    def weights_second():
        for step in range(1, nx):
            down_first(step).wait()
        down_start()
        for step in range(1, ny):
            up_first(step).wait()
        up_start()

    def count_chunk(chunk):
        at = pl.ds(pl.multiple_of(chunk * samples, LANES), samples)
        slots = jnp.concatenate([slots_ref[0, :, at], slots_ref[1, :, at]], axis=1)
        low = lax.bitwise_and(slots, LANES - 1)
        high = lax.shift_right_logical(slots, 7)
        unit = lax.shift_left(jnp.ones_like(high), 4 * lax.bitwise_and(high, 7))
        parts = [jnp.where(lax.shift_right_logical(high, 3) == k, unit, 0) for k in range(words)]

        def rows_step(q):
            ids = lax.broadcasted_iota(jnp.int32, (16, 2 * samples), 0) + q * 16
            total = [jnp.zeros((16, 2 * samples), jnp.int32) for _ in range(words)]
            for l in range(pool):
                hit = ids == low[l : l + 1, :]
                for k in range(words):
                    total[k] = total[k] + jnp.where(hit, parts[k][l : l + 1, :], 0)
            for h in range(his):
                digit = lax.bitwise_and(lax.shift_right_logical(total[h // 8], 4 * (h % 8)), 15)
                counts[chunk, pl.ds(pl.multiple_of(h * LANES + q * 16, 16), 16), :] = digit.astype(F32).astype(BF)

        each(0, LANES // 16, rows_step)

    def chunk_of(index):
        return lax.rem(grp + order[index], n_grp)

    def hot_pool(chunk):
        pooled_hot[chunk] = jnp.dot(
            buffer_t[:, :hot_count], counts[chunk, :hot_count, :], preferred_element_type=F32
        )

    early = (3 * n_grp) // 8
    for index in range(early):
        count_chunk(chunk_of(index))
    weights_second()
    cold_bf[...] = cold_ref[...].astype(BF)

    each(1, n_wide, lambda step: ask_from(lax.rem(me + step, n_wide)).wait_recv())
    per_batch = LANES // cap

    def batch_step(batch):
        spread = jnp.concatenate(
            [jnp.broadcast_to(asked[batch * per_batch + k], (cap, LANES)) for k in range(per_batch)], axis=0
        ).astype(F32)
        lane = lax.broadcasted_iota(jnp.int32, (LANES, LANES), 1)
        row = lax.broadcasted_iota(jnp.int32, (LANES, LANES), 0)
        kept = jnp.where(lane == lax.rem(row, cap), spread, 0.0)
        wanted = jnp.sum(kept, axis=1, keepdims=True).astype(jnp.int32)
        asked_lane[pl.ds(batch, 1), :] = jnp.sum(jnp.transpose(kept), axis=0, keepdims=True).astype(jnp.int32)
        hit = lax.broadcasted_iota(jnp.int32, (LANES, owned), 1) == wanted
        rows = jnp.dot(jnp.where(hit, 1.0, 0.0).astype(BF), cold_bf[...], preferred_element_type=F32).astype(BF)
        for k in range(per_batch):
            picked[batch * per_batch + k] = rows[k * cap : (k + 1) * cap]

    each(0, n_wide // per_batch, batch_step)

    def row_copy(other):
        return push(picked.at[other], fetched.at[me], row_send.at[other], row_recv.at[me], {"wide": other})

    def row_from(other):
        return push(picked.at[me], fetched.at[other], row_send.at[me], row_recv.at[other], {"wide": other})

    each(1, n_wide, lambda step: row_copy(lax.rem(me + step, n_wide)).start())
    fetched[me] = picked[me]

    stacked[:, :width] = dense_ref[...]
    for k in range(hot_count // LANES):
        buffer_t[:, k * LANES : (k + 1) * LANES] = jnp.transpose(hot_ref[k * LANES : (k + 1) * LANES, :]).astype(BF)
    serve = [list(down_serve), list(up_serve)]

    def serve_next(which):
        if serve[which]:
            serve[which].pop(0)()

    for index in range(n_grp):
        chunk = chunk_of(index)
        if index >= early:
            count_chunk(chunk)
        hot_pool(chunk)
        if index == n_grp // 2:
            serve_next(0)
    serve_next(1)
    serve_next(0)

    def fill(batch):
        ids = lax.broadcasted_iota(jnp.int32, (owned, LANES), 0)
        chosen[:, pl.ds(pl.multiple_of(batch * LANES, LANES), LANES)] = jnp.where(
            ids == asked_lane[pl.ds(batch, 1), :], 1.0, 0.0
        ).astype(BF)

    each(0, chosen.shape[1] // LANES, fill)

    def row_wait(step):
        other = lax.rem(me + step, n_wide)
        row_from(other).wait_recv()
        row_copy(other).wait_send()
        ask_copy(other).wait_send()

    each(1, n_wide, row_wait)
    for k in range((slot_total - hot_count) // LANES):
        part = jnp.concatenate([fetched[k * per_batch + i] for i in range(per_batch)], axis=0).astype(F32)
        at = hot_count + k * LANES
        buffer_t[:, at : at + LANES] = jnp.transpose(part).astype(BF)

    def table_lanes(owner):
        return pl.ds(pl.multiple_of(width + 2 * width * owner, LANES), 2 * width)

    def pooled_copy(other):
        return push(pooled_out.at[other], stacked.at[:, table_lanes(grp)], p_send.at[other], p_recv.at[grp], {"grp": other})

    def pooled_from(other):
        return push(pooled_out.at[grp], stacked.at[:, table_lanes(other)], p_send.at[grp], p_recv.at[other], {"grp": other})

    for index in range(n_grp):
        chunk = chunk_of(index)
        pooled_t = pooled_hot[chunk] + jnp.dot(
            buffer_t[:, hot_count:], counts[chunk, hot_count:, :], preferred_element_type=F32
        )
        for t in range(2):
            pooled_out[chunk, :, t * width : (t + 1) * width] = jnp.transpose(
                pooled_t[:, t * samples : (t + 1) * samples]
            ).astype(BF)
        if index < n_grp - 1:
            pooled_copy(chunk).start()
    stacked[:, table_lanes(grp)] = pooled_out[grp]

    while serve[0] or serve[1]:
        serve_next(0)
        serve_next(1)
    down_drain()
    up_drain()
    down_size = rank // LANES * down_rows

    def down_shard(w):
        shard32[...] = all_down[lax.rem(w // nc, ny), lax.rem(w, nc), w // (nc * ny)].astype(F32)
        for j in range(rank // LANES):
            down32[j, pl.ds(w * down_rows, down_rows), :] = shard32[j * down_rows : (j + 1) * down_rows, :]

    each(0, n_wide, down_shard)

    def down_round(i):
        at = pl.ds(pl.multiple_of(i * LANES, LANES), LANES)
        for j in range(rank // LANES):
            down[at, j * LANES : (j + 1) * LANES] = down32[j, at, :].astype(BF)

    each(0, columns // LANES, down_round)

    def up_shard(q):
        both = [all_up[q // ny, c, lax.rem(q, ny)].astype(F32) for c in range(nc)]
        for j in range(columns // LANES):
            up[pl.ds(pl.multiple_of(q * nc * up_rows, nc * up_rows), nc * up_rows), j * LANES : (j + 1) * LANES] = (
                jnp.concatenate([part[j * up_rows : (j + 1) * up_rows] for part in both], axis=0).astype(BF)
            )

    each(0, chips, up_shard)

    for index in range(n_grp - 1):
        pooled_copy(chunk_of(index)).wait_send()
        pooled_from(lax.rem(grp + n_grp - order[index], n_grp)).wait_recv()

    def bias_at(at):
        return small_ref[:, at]

    def head_at(start, size):
        if isinstance(start, int):
            return small_ref[:, columns + start : columns + start + size]
        return small_ref[:, pl.ds(pl.multiple_of(columns + start, LANES), size)]

    low_rank = jnp.dot(stacked[...], down[...], preferred_element_type=F32).astype(BF)
    partial = jnp.zeros((samples, LANES), F32)
    for k in range(columns // LANES):
        at = slice(k * LANES, (k + 1) * LANES)
        wide = stacked[:, at].astype(F32)
        part = jnp.dot(low_rank, up[:, at], preferred_element_type=F32) + bias_at(at)
        gain[:, at] = part
        partial = partial + (wide * part + wide) * head_at(k * LANES, LANES)
    logits = jnp.sum(jnp.transpose(partial), axis=0, keepdims=True)
    logits_ref[...] = logits
    residual = jax.nn.sigmoid(logits) - small_ref[:, 2 * columns :]
    residual = jnp.transpose(jnp.broadcast_to(residual, (LANES, samples)))
    low_grad = jnp.zeros((samples, rank), F32)
    for k in range(columns // LANES):
        at = slice(k * LANES, (k + 1) * LANES)
        d_crossed = residual * head_at(k * LANES, LANES)
        d_gain = (d_crossed * stacked[:, at].astype(F32)).astype(BF)
        low_grad = low_grad + lax.dot_general(
            d_gain, up[:, at], (((1,), (1,)), ((), ())), preferred_element_type=F32
        )
    d_low[...] = low_grad.astype(BF)

    def d_copy(other):
        return push(d_out.at[other], d_in.at[grp], g_send.at[other], g_recv.at[grp], {"grp": other})

    def d_from(other):
        return push(d_out.at[grp], d_in.at[other], g_send.at[grp], g_recv.at[other], {"grp": other})

    for index in range(n_grp):
        other = chunk_of(index)
        at = table_lanes(other)
        back = lax.dot_general(
            d_low[...], down[at, :], (((1,), (1,)), ((), ())), preferred_element_type=F32
        )
        d_crossed = jnp.concatenate([residual, residual], axis=1) * head_at(width + 2 * width * other, 2 * width)
        d_out[other] = (d_crossed * (gain[:, at] + 1.0) + back).astype(BF)
        if index < n_grp - 1:
            d_copy(other).start()
    d_in[grp] = d_out[grp]

    tile = 4 * LANES if slot_total % (4 * LANES) == 0 else LANES

    def grad_chunk(chunk, first, last):
        both = d_in[chunk]
        d_rows = jnp.concatenate([both[:, :width], both[:, width:]], axis=0)

        def tile_step(i):
            at = pl.ds(pl.multiple_of(i * tile, tile), tile)
            part = jnp.dot(counts[chunk, at, :], d_rows, preferred_element_type=F32)
            slot_grad[at, :] = part if first else slot_grad[at, :] + part

        each(0, slot_total // tile, tile_step)

    grad_chunk(grp, True, n_grp == 1)
    for index in range(n_grp - 1):
        other = lax.rem(grp + n_grp - order[index], n_grp)
        d_copy(chunk_of(index)).wait_send()
        d_from(other).wait_recv()
        grad_chunk(other, False, index == n_grp - 2)
    hot_grad[...] = slot_grad[:hot_count, :].astype(BF)
    cold_grad[...] = slot_grad[hot_count:, :].astype(BF).reshape(cold_grad.shape)

    per_half = hot_count // 2
    per_chip = per_half // chips

    def half_at(c):
        return pl.ds(pl.multiple_of(c * per_half, per_half), per_half)

    def chip_at(q):
        return pl.ds(pl.multiple_of(q * per_chip, per_chip), per_chip)

    pair = push(hot_grad.at[half_at(1 - core)], pair_in, pair_send, pair_recv, sibling)
    pair.start()

    def cold_copy(other):
        return push(cold_grad.at[other], cold_in.at[me], c_send.at[other], c_recv.at[me], {"wide": other})

    def cold_from(other):
        return push(cold_grad.at[me], cold_in.at[other], c_send.at[me], c_recv.at[other], {"wide": other})

    def rs_copy(q):
        return push(half.at[chip_at(q)], rs_in.at[chip], rs_send.at[q], rs_recv.at[chip], {"wide": q * nc + core})

    def rs_from(q):
        return push(half.at[chip_at(q)], rs_in.at[q], rs_send.at[q], rs_recv.at[q], {"wide": q * nc + core})

    pair.wait()
    half[...] = (hot_grad[half_at(core), :].astype(F32) + pair_in[...].astype(F32)).astype(BF)
    each(1, chips, lambda step: rs_copy(lax.rem(chip + step, chips)).start())
    rs_in[chip] = half[chip_at(chip), :]
    each(1, n_wide, lambda step: cold_copy(lax.rem(me + step, n_wide)).start())
    cold_in[me] = cold_grad[me]

    def rs_wait(step):
        q = lax.rem(chip + step, chips)
        rs_from(q).wait_recv()
        rs_copy(q).wait_send()

    each(1, chips, rs_wait)

    def own_at(q):
        return pl.ds(pl.multiple_of(core * per_half + q * per_chip, per_chip), per_chip)

    summed = lax.fori_loop(
        0, chips, lambda q, so_far: so_far + rs_in[q].astype(F32), jnp.zeros((per_chip, LANES), F32)
    )
    total_ref[own_at(chip), :] = summed.astype(BF)

    def ag_copy(q):
        mine = total_ref.at[own_at(chip)]
        return push(mine, mine, ag_send.at[q], ag_recv.at[chip], {"wide": q * nc + core})

    def ag_from(q):
        theirs = total_ref.at[own_at(q)]
        return push(theirs, theirs, ag_send.at[q], ag_recv.at[q], {"wide": q * nc + core})

    each(1, chips, lambda step: ag_copy(lax.rem(chip + step, chips)).start())

    def cold_wait(step):
        other = lax.rem(me + step, n_wide)
        cold_from(other).wait_recv()
        cold_copy(other).wait_send()

    each(1, n_wide, cold_wait)
    cold_sum_ref[...] = jnp.dot(
        chosen[...], cold_in[...].reshape(chosen.shape[1], LANES), preferred_element_type=F32
    )

    def ag_wait(step):
        q = lax.rem(chip + step, chips)
        ag_from(q).wait_recv()
        ag_copy(q).wait_send()

    each(1, chips, ag_wait)
    side = push(total_ref.at[half_at(core)], total_ref.at[half_at(core)], sib_send, sib_recv, sibling)
    side.start()
    side.wait()


def adagrad_kernel(
    logits_in, hot_grad, cold_grad, hot_ref, hot_accum, cold_ref, cold_accum,
    logits_ref, new_hot, new_hot_accum, new_cold, new_cold_accum,
):
    logits_ref[...] = logits_in[...]
    for grad_ref, rows_ref, accum_ref, new_rows, new_accum in (
        (hot_grad, hot_ref, hot_accum, new_hot, new_hot_accum),
        (cold_grad, cold_ref, cold_accum, new_cold, new_cold_accum),
    ):
        for start in range(0, rows_ref.shape[0], LANES):
            at = slice(start, start + LANES)
            gradient = grad_ref[at, :].astype(F32)
            square = jnp.sum(jnp.transpose(gradient * gradient), axis=0, keepdims=True)
            accum = accum_ref[:, at] + square / LANES
            new_accum[:, at] = accum
            scale = jnp.transpose(jnp.broadcast_to(jnp.sqrt(accum) + EPSILON, (LANES, LANES)))
            new_rows[at, :] = rows_ref[at, :] - LEARN * gradient / scale


VMEM = pl.BlockSpec(memory_space=pltpu.VMEM)
DMA = pltpu.SemaphoreType.DMA


def on_device(
    n_wide, n_grp,
    dense_features, bag_slots, cold_offset, hot_rows, hot_accum, cold_rows, cold_accum,
    cross_down, cross_up, cross_bias, out_weight, labels,
):
    nx, ny, nc = wide_shape(n_wide)
    chips = nx * ny
    samples, width = dense_features.shape
    hot_count = hot_rows.shape[1]
    owned = cold_rows.shape[1]
    cap = cold_offset.shape[3]
    requests = n_wide * cap
    slot_total = hot_count + requests
    down_rows, rank = cross_down.shape
    up_rows, columns = cross_up.shape
    shard_rows = round_up(max(down_rows * rank, up_rows * columns) // LANES, 16)
    slots = jnp.transpose(bag_slots, (0, 2, 1))
    small = jnp.concatenate([cross_bias, out_weight.astype(F32), labels.astype(F32)]).reshape(1, -1)

    def vm(*shape, dtype=BF):
        return pltpu.VMEM(shape, dtype)

    logits, hot_grad, cold_grad = pl.pallas_call(
        functools.partial(step_kernel, n_wide, n_grp),
        out_shape=(
            jax.ShapeDtypeStruct((1, samples), F32),
            jax.ShapeDtypeStruct((hot_count, width), BF),
            jax.ShapeDtypeStruct((owned, width), F32),
        ),
        in_specs=[VMEM] * 8,
        out_specs=(VMEM,) * 3,
        scratch_shapes=[
            vm(n_wide, 1, LANES, dtype=jnp.int32), vm(n_wide, 1, LANES, dtype=jnp.int32),
            vm(requests // LANES, LANES, dtype=jnp.int32),
            vm(owned, width), vm(n_wide, cap, width), vm(n_wide, cap, width),
            vm(shard_rows, LANES, dtype=F32), vm(shard_rows, LANES), vm(shard_rows, LANES),
            vm(ny, nc, nx, shard_rows, LANES), vm(nx, nc, ny, shard_rows, LANES),
            vm(rank // LANES, columns, LANES, dtype=F32), vm(columns, rank), vm(rank, columns),
            vm(width, slot_total), vm(n_grp, slot_total, 2 * samples),
            vm(n_grp, width, 2 * samples, dtype=F32), vm(n_grp, samples, 2 * width),
            vm(samples, columns), vm(samples, columns, dtype=F32), vm(samples, rank),
            vm(n_grp, samples, 2 * width), vm(n_grp, samples, 2 * width), vm(slot_total, width, dtype=F32),
            vm(hot_count, width), vm(n_wide, cap, width), vm(n_wide, cap, width),
            vm(hot_count // 2, width), vm(hot_count // 2, width), vm(chips, hot_count // 2 // chips, width),
            vm(owned, requests),
            DMA((n_wide,)), DMA((n_wide,)), DMA((n_wide,)), DMA((n_wide,)),
            DMA((nx,)), DMA((nx,)), DMA((ny,)), DMA((ny,)), DMA((ny,)), DMA((ny,)), DMA((ny,)), DMA((ny,)),
            DMA((ny,)), DMA((ny,)), DMA((nx,)), DMA((nx,)), DMA((nx,)), DMA((nx,)), DMA((nx,)), DMA((nx,)),
            DMA((n_grp,)), DMA((n_grp,)), DMA((n_grp,)), DMA((n_grp,)),
            DMA((n_wide,)), DMA((n_wide,)), DMA, DMA,
            DMA((chips,)), DMA((chips,)), DMA((chips,)), DMA((chips,)), DMA, DMA,
        ],
        compiler_params=pltpu.CompilerParams(
            collective_id=0, has_side_effects=True, vmem_limit_bytes=60 * 1024 * 1024
        ),
        name="train_step",
    )(cold_offset[0, 0], cold_rows[0], cross_down, cross_up, slots, hot_rows[0], dense_features, small)

    steps = 8 if hot_count % (8 * LANES) == 0 and owned % (8 * LANES) == 0 else 1
    hot_block, cold_block = hot_count // steps, owned // steps

    def rows_spec(size):
        return pl.BlockSpec((size, width), lambda i: (i, 0))

    def accum_spec(size):
        return pl.BlockSpec((1, size), lambda i: (0, i))

    whole = pl.BlockSpec((1, samples), lambda i: (0, 0))
    logits, new_hot, new_hot_accum, new_cold, new_cold_accum = pl.pallas_call(
        adagrad_kernel,
        grid=(steps,),
        out_shape=(
            jax.ShapeDtypeStruct((1, samples), F32),
            jax.ShapeDtypeStruct((hot_count, width), F32),
            jax.ShapeDtypeStruct((1, hot_count), F32),
            jax.ShapeDtypeStruct((owned, width), F32),
            jax.ShapeDtypeStruct((1, owned), F32),
        ),
        in_specs=[
            whole, rows_spec(hot_block), rows_spec(cold_block),
            rows_spec(hot_block), accum_spec(hot_block), rows_spec(cold_block), accum_spec(cold_block),
        ],
        out_specs=(whole, rows_spec(hot_block), accum_spec(hot_block), rows_spec(cold_block), accum_spec(cold_block)),
        name="adagrad",
    )(logits, hot_grad, cold_grad, hot_rows[0], hot_accum, cold_rows[0], cold_accum)
    return (logits.reshape(samples), new_hot[None], new_hot_accum, new_cold[None], new_cold_accum)


def solution(mesh):
    return jax.shard_map(
        functools.partial(on_device, mesh.shape["wide"], mesh.shape["grp"]),
        mesh=mesh,
        in_specs=(
            P(("wide", "grp"), None),
            P("grp", "wide", None),
            P("grp", "wide", None, None),
            P("grp", None, None),
            P("grp", None),
            P("grp", "wide", None),
            P("grp", "wide"),
            P("wide", None),
            P("wide", None),
            P(),
            P(),
            P(("wide", "grp")),
        ),
        out_specs=(
            P(("wide", "grp")),
            P("grp", None, None),
            P("grp", None),
            P("grp", "wide", None),
            P("grp", "wide"),
        ),
        check_vma=False,
    )
```

```python
import functools

import jax
import jax.numpy as jnp
from jax import lax
from jax.experimental import pallas as pl
from jax.experimental.pallas import tpu as pltpu
from jax.sharding import PartitionSpec as P

LEARN = 0.1
EPSILON = 1e-08
LANES = 128
GRADIENT_TILE = 1024
GRADIENT_PARTS = {8: [(7, 8), (0, 3), (3, 7)], 2: [(1, 2), (0, 1)]}
BF = jnp.bfloat16
F32 = jnp.float32


def wide_shape(n_wide):
    return {64: (4, 8, 2), 8: (2, 2, 2)}[n_wide]


def round_up(value, unit):
    return -(-value // unit) * unit


def push(src, dst, send_sem, recv_sem, target):
    return pltpu.make_async_remote_copy(
        src_ref=src,
        dst_ref=dst,
        send_sem=send_sem,
        recv_sem=recv_sem,
        device_id=target,
        device_id_type=pl.DeviceIdType.MESH,
    )


def each(first, last, body):
    def step(i, carry):
        body(i)
        return carry

    lax.fori_loop(first, last, step, 0)


def far_first(count):
    return sorted(range(1, count), key=lambda o: -min(o, count - o)) + [0]


def step_kernel(
    n_wide, n_grp,
    offset_ref, cold_hbm, down_ref, up_ref, slots_ref, hot_hbm, dense_ref, bias_ref, head_ref, labels_ref,
    logits_ref, total_ref, cold_sum_ref,
    cold_ref, hot_ref, small, square, ask, asked, asked_lane, cold_bf, picked, fetched,
    shard32, shard_down, shard_up, all_down, all_up, down32, down, up,
    buffer_t, counts, pooled_hot, pooled_out, stacked, gain, d_low, d_out, d_in, slot_grad,
    hot_grad, cold_grad, cold_in, pair_in, half, x_in, quarter, y_in, chosen,
    load_sem, ask_sem, row_sem, d1_sem, u1_sem, p_sem, c_sem, pair_sem, xrs_sem, yrs_sem, yag_sem,
    d_send, d_fwd, d_bwd, d_side, u_send, u_fwd, u_bwd, u_side, g_send, g_recv, xag_send, xag_recv, sib_send, sib_recv,
):
    nx, ny, nc = wide_shape(n_wide)
    chips = nx * ny
    me = lax.axis_index("wide")
    grp = lax.axis_index("grp")
    core = lax.rem(me, nc)
    chip = me // nc
    y = lax.rem(chip, ny)
    x = chip // ny
    sibling = {"wide": me + 1 - 2 * core}
    hot_count, width = hot_ref.shape
    owned = cold_ref.shape[0]
    cap = picked.shape[1]
    slot_total = buffer_t.shape[1]
    samples = dense_ref.shape[0]
    columns = stacked.shape[1]
    his = slot_total // LANES
    words = -(-his // 8)
    pool = slots_ref.shape[1]
    order = far_first(n_grp)

    def at_wide(x_, y_):
        return {"wide": (x_ * ny + y_) * nc + core}

    def bytes_of(ref, sems):
        return push(ref, ref, sems.at[0], sems.at[1], sibling)

    loads = [
        pltpu.make_async_copy(cold_hbm, cold_ref, load_sem.at[0]),
        pltpu.make_async_copy(hot_hbm, hot_ref, load_sem.at[1]),
    ]
    for load in loads:
        load.start()

    barrier = pltpu.get_barrier_semaphore()
    for axis, count, mine in (("wide", n_wide, me), ("grp", n_grp, grp)):
        each(1, count, lambda step: pl.semaphore_signal(
            barrier, inc=1, device_id={axis: lax.rem(mine + step, count)}, device_id_type=pl.DeviceIdType.MESH
        ))

    square[...] = jnp.zeros_like(square)
    square[:cap, :n_wide] = offset_ref[...].astype(F32)
    ask[...] = jnp.transpose(square[...])[:n_wide]
    for k in range(columns // LANES):
        at = slice(k * LANES, (k + 1) * LANES)
        small[:, at] = bias_ref[at].reshape(1, LANES)
        small[:, columns + k * LANES : columns + (k + 1) * LANES] = head_ref[at].astype(F32).reshape(1, LANES)
    small[:, 2 * columns :] = labels_ref[...].astype(F32).reshape(1, samples)
    down_rows, rank = down_ref.shape
    up_rows = up_ref.shape[0]
    shard32[...] = jnp.zeros_like(shard32)
    for j in range(rank // LANES):
        shard32[j * down_rows : (j + 1) * down_rows, :] = down_ref[:, j * LANES : (j + 1) * LANES].astype(F32)
    shard_down[...] = shard32[...].astype(BF)
    for j in range(columns // LANES):
        shard32[j * up_rows : (j + 1) * up_rows, :] = up_ref[:, j * LANES : (j + 1) * LANES].astype(F32)
    shard_up[...] = shard32[...].astype(BF)
    all_down[y, core, x] = shard_down[...]
    all_up[x, core, y] = shard_up[...]
    pl.semaphore_wait(barrier, n_wide + n_grp - 2)

    def row_of(index):
        return pl.ds(index, 1)

    def ask_copy(other):
        return push(ask.at[row_of(other)], asked.at[row_of(me)], ask_sem.at[0], ask_sem.at[1], {"wide": other})

    each(1, n_wide, lambda step: ask_copy(lax.rem(me + step, n_wide)).start())
    asked[row_of(me), :] = ask[row_of(me), :]

    for step in far_first(nx)[:-1]:
        push(
            shard_down, all_down.at[y, core, x], d1_sem.at[0], d1_sem.at[1], at_wide(lax.rem(x + step, nx), y)
        ).start()
    for step in far_first(ny)[:-1]:
        push(
            shard_up, all_up.at[x, core, y], u1_sem.at[0], u1_sem.at[1], at_wide(x, lax.rem(y + step, ny))
        ).start()

    def ring(blocks, mine, length, place, send, fwd_recv, bwd_recv, side_recv):
        n_fwd, n_bwd = length // 2, (length - 1) // 2

        def index(step):
            return lax.rem(mine + length - step, length)

        def fwd(step):
            held = blocks.at[index(step), core]
            return push(held, held, send.at[0], fwd_recv.at[step], place(lax.rem(mine + 1, length)))

        def bwd(step):
            held = blocks.at[lax.rem(mine + step, length), core]
            return push(held, held, send.at[1], bwd_recv.at[step], place(lax.rem(mine + length - 1, length)))

        def side(step):
            held = blocks.at[index(step), core]
            return push(held, held, send.at[2], side_recv.at[step], sibling)

        def start():
            fwd(0).start()
            if n_bwd:
                bwd(0).start()
            side(0).start()

        def serve(step):
            fwd(step).wait_recv()
            if step + 1 < n_fwd:
                fwd(step + 1).start()
            side(step + 1).start()
            if step < n_bwd:
                bwd(step).wait_recv()
                if step + 1 < n_bwd:
                    bwd(step + 1).start()
                side(length - step - 1).start()

        def ready(step):
            side(step).wait_recv()
            return index(step)

        def drain():
            for which, count in enumerate((n_fwd, n_bwd, length)):
                if count:
                    held = blocks.at[pl.ds(0, count), core]
                    push(held, held, send.at[which], side_recv.at[0], sibling).wait_send()

        steps = [[0]] + [[step + 1] + ([length - step - 1] if step < n_bwd else []) for step in range(n_fwd)]
        return start, serve, ready, drain, steps

    down_start, down_serve, down_ready, down_drain, down_steps = ring(
        all_down, y, ny, lambda row: at_wide(x, row), d_send, d_fwd, d_bwd, d_side
    )
    up_start, up_serve, up_ready, up_drain, up_steps = ring(
        all_up, x, nx, lambda row: at_wide(row, y), u_send, u_fwd, u_bwd, u_side
    )

    def down_rows_of(row):
        def shard(i):
            x_, c = i // nc, lax.rem(i, nc)
            shard32[...] = all_down[row, c, x_].astype(F32)
            first = ((x_ * ny + row) * nc + c) * down_rows
            for j in range(rank // LANES):
                down32[j, pl.ds(first, down_rows), :] = shard32[j * down_rows : (j + 1) * down_rows, :]

        each(0, nx * nc, shard)

    def up_rows_of(x_):
        def pair_of(y_):
            both = [all_up[x_, c, y_].astype(F32) for c in range(nc)]
            first = pl.multiple_of((x_ * ny + y_) * nc * up_rows, nc * up_rows)
            for j in range(columns // LANES):
                up[pl.ds(first, nc * up_rows), j * LANES : (j + 1) * LANES] = jnp.concatenate(
                    [part[j * up_rows : (j + 1) * up_rows] for part in both], axis=0
                ).astype(BF)

        each(0, ny, pair_of)

    def serve_down(step):
        if step < len(down_steps) - 1:
            down_serve(step)

    def serve_up(step):
        if step < len(up_steps) - 1:
            up_serve(step)

    def lay_down(step):
        for block in down_steps[step] if step < len(down_steps) else []:
            down_rows_of(down_ready(block))

    def lay_up(step):
        for block in up_steps[step] if step < len(up_steps) else []:
            up_rows_of(up_ready(block))

    def chunk_of(index):
        return lax.rem(grp + order[index], n_grp)

    def lanes_of(first, last):
        return slice(first * 2 * samples, last * 2 * samples)

    def count_chunk(index):
        chunk = chunk_of(index)
        at = pl.ds(pl.multiple_of(chunk * samples, LANES), samples)
        slots = jnp.concatenate([slots_ref[0, :, at], slots_ref[1, :, at]], axis=1)
        low = lax.bitwise_and(slots, LANES - 1)
        high = lax.shift_right_logical(slots, 7)
        unit = lax.shift_left(jnp.ones_like(high), 4 * lax.bitwise_and(high, 7))
        parts = [jnp.where(lax.shift_right_logical(high, 3) == k, unit, 0) for k in range(words)]

        def rows_step(q):
            ids = lax.broadcasted_iota(jnp.int32, (16, 2 * samples), 0) + q * 16
            total = [jnp.zeros((16, 2 * samples), jnp.int32) for _ in range(words)]
            for l in range(pool):
                hit = ids == low[l : l + 1, :]
                for k in range(words):
                    total[k] = total[k] + jnp.where(hit, parts[k][l : l + 1, :], 0)
            for h in range(his):
                digit = lax.bitwise_and(lax.shift_right_logical(total[h // 8], 4 * (h % 8)), 15)
                counts[pl.ds(pl.multiple_of(h * LANES + q * 16, 16), 16), lanes_of(index, index + 1)] = digit.astype(F32).astype(BF)

        each(0, LANES // 16, rows_step)

    def hot_pool(index):
        pooled_hot[index] = jnp.dot(
            buffer_t[:, :hot_count], counts[:hot_count, lanes_of(index, index + 1)], preferred_element_type=F32
        )

    early = (3 * n_grp) // 8
    for index in range(early):
        count_chunk(index)
    loads[0].wait()
    cold_bf[...] = cold_ref[...].astype(BF)
    bytes_of(all_down.at[y, core, pl.ds(0, nx - 1)], d1_sem).wait()
    down_start()

    asks = bytes_of(ask.at[pl.ds(0, n_wide - 1)], ask_sem)
    asks.wait_recv()
    per_batch = LANES // cap

    batches = n_wide // per_batch

    def batch_step(step):
        batch = lax.rem(me // per_batch + step, batches)
        spread = jnp.concatenate(
            [jnp.broadcast_to(asked[row_of(batch * per_batch + k), :], (cap, LANES)) for k in range(per_batch)], axis=0
        )
        lane = lax.broadcasted_iota(jnp.int32, (LANES, LANES), 1)
        row = lax.broadcasted_iota(jnp.int32, (LANES, LANES), 0)
        kept = jnp.where(lane == lax.rem(row, cap), spread, 0.0)
        wanted = jnp.sum(kept, axis=1, keepdims=True).astype(jnp.int32)
        asked_lane[pl.ds(batch, 1), :] = jnp.sum(jnp.transpose(kept), axis=0, keepdims=True).astype(jnp.int32)
        hit = lax.broadcasted_iota(jnp.int32, (LANES, owned), 1) == wanted
        rows = jnp.dot(jnp.where(hit, 1.0, 0.0).astype(BF), cold_bf[...], preferred_element_type=F32).astype(BF)
        for k in range(per_batch):
            other = batch * per_batch + k
            picked[other] = rows[k * cap : (k + 1) * cap]

            @pl.when(other != me)
            def _():
                push(
                    picked.at[other], fetched.at[me], row_sem.at[0], row_sem.at[1], {"wide": other}
                ).start()

    each(0, batches, batch_step)
    fetched[me] = picked[me]
    bytes_of(all_up.at[x, core, pl.ds(0, ny - 1)], u1_sem).wait()
    up_start()
    serve_down(0)

    stacked[:, :width] = dense_ref[...]
    loads[1].wait()
    for k in range(hot_count // LANES):
        buffer_t[:, k * LANES : (k + 1) * LANES] = jnp.transpose(hot_ref[k * LANES : (k + 1) * LANES, :]).astype(BF)
    for index in range(n_grp):
        if index >= early:
            count_chunk(index)
        hot_pool(index)

    def fill(batch):
        ids = lax.broadcasted_iota(jnp.int32, (owned, LANES), 0)
        chosen[:, pl.ds(pl.multiple_of(batch * LANES, LANES), LANES)] = jnp.where(
            ids == asked_lane[pl.ds(batch, 1), :], 1.0, 0.0
        ).astype(BF)

    asks.wait_send()
    rows_moved = bytes_of(picked.at[pl.ds(0, n_wide - 1)], row_sem)
    rows_moved.wait_recv()
    for k in range((slot_total - hot_count) // LANES):
        part = jnp.concatenate([fetched[k * per_batch + i] for i in range(per_batch)], axis=0).astype(F32)
        at = hot_count + k * LANES
        buffer_t[:, at : at + LANES] = jnp.transpose(part).astype(BF)

    def table_lanes(owner):
        return pl.ds(pl.multiple_of(width + 2 * width * owner, LANES), 2 * width)

    for index in range(n_grp):
        chunk = chunk_of(index)
        pooled_t = pooled_hot[index] + jnp.dot(
            buffer_t[:, hot_count:], counts[hot_count:, lanes_of(index, index + 1)], preferred_element_type=F32
        )
        for t in range(2):
            pooled_out[chunk, :, t * width : (t + 1) * width] = jnp.transpose(
                pooled_t[:, t * samples : (t + 1) * samples]
            ).astype(BF)
        if index < n_grp - 1:
            push(
                pooled_out.at[chunk], stacked.at[:, table_lanes(grp)], p_sem.at[0], p_sem.at[1], {"grp": chunk}
            ).start()
    stacked[:, table_lanes(grp)] = pooled_out[grp]

    for step in range(len(down_steps)):
        serve_down(step + 1)
        if step == len(down_steps) - 2:
            each(0, chosen.shape[1] // LANES, fill)
        serve_up(step)
        lay_up(step)
        lay_down(step)
    up_drain()
    down_drain()

    def down_round(i):
        at = pl.ds(pl.multiple_of(i * LANES, LANES), LANES)
        for j in range(rank // LANES):
            down[at, j * LANES : (j + 1) * LANES] = down32[j, at, :].astype(BF)

    each(0, columns // LANES, down_round)
    rows_moved.wait_send()
    bytes_of(stacked.at[:, width : width + 2 * width * (n_grp - 1)], p_sem).wait()

    def bias_at(at):
        return small[:, at]

    def head_at(start, size):
        if isinstance(start, int):
            return small[:, columns + start : columns + start + size]
        return small[:, pl.ds(pl.multiple_of(columns + start, LANES), size)]

    low_rank = jnp.dot(stacked[...], down[...], preferred_element_type=F32).astype(BF)
    partial = jnp.zeros((samples, LANES), F32)
    for k in range(columns // LANES):
        at = slice(k * LANES, (k + 1) * LANES)
        wide = stacked[:, at].astype(F32)
        part = jnp.dot(low_rank, up[:, at], preferred_element_type=F32) + bias_at(at)
        gain[:, at] = part
        partial = partial + (wide * part + wide) * head_at(k * LANES, LANES)
    logits = jnp.sum(jnp.transpose(partial), axis=0, keepdims=True)
    logits_ref[...] = logits
    residual = jax.nn.sigmoid(logits) - small[:, 2 * columns :]
    residual = jnp.transpose(jnp.broadcast_to(residual, (LANES, samples)))
    low_grad = jnp.zeros((samples, rank), F32)
    for k in range(columns // LANES):
        at = slice(k * LANES, (k + 1) * LANES)
        d_crossed = residual * head_at(k * LANES, LANES)
        d_gain = (d_crossed * stacked[:, at].astype(F32)).astype(BF)
        low_grad = low_grad + lax.dot_general(
            d_gain, up[:, at], (((1,), (1,)), ((), ())), preferred_element_type=F32
        )
    d_low[...] = low_grad.astype(BF)

    def place_of(index):
        return order.index((n_grp - order[index]) % n_grp)

    def lying(index):
        return d_in.at[pl.ds(index * 2 * samples, 2 * samples)]

    for index in range(n_grp):
        other = chunk_of(index)
        at = table_lanes(other)
        back = lax.dot_general(
            d_low[...], down[at, :], (((1,), (1,)), ((), ())), preferred_element_type=F32
        )
        d_crossed = jnp.concatenate([residual, residual], axis=1) * head_at(width + 2 * width * other, 2 * width)
        d_both = (d_crossed * (gain[:, at] + 1.0) + back).astype(BF)
        if index < n_grp - 1:
            place = place_of(index)
            d_out[index, :samples] = d_both[:, :width]
            d_out[index, samples:] = d_both[:, width:]
            push(d_out.at[index], lying(place), g_send, g_recv.at[place], {"grp": other}).start()
        else:
            d_in[index * 2 * samples : index * 2 * samples + samples] = d_both[:, :width]
            d_in[index * 2 * samples + samples :] = d_both[:, width:]

    parts = GRADIENT_PARTS[n_grp]

    def grad_rows(start, stop, part, first, last, out):
        def tile_step(at):
            lanes = lanes_of(*part)
            total = jnp.dot(counts[at, lanes], d_in[lanes, :], preferred_element_type=F32)
            if not first:
                total = slot_grad[at, :] + total
            if last:
                out(at, total.astype(BF))
            else:
                slot_grad[at, :] = total

        for begin in range(start, stop, GRADIENT_TILE):
            tile_step(slice(begin, min(stop, begin + GRADIENT_TILE)))

    def hot_done(at, value):
        hot_grad[at, :] = value

    def cold_done(at, value):
        rows = slice((at.start - hot_count) // cap, (at.stop - hot_count) // cap)
        cold_grad[rows] = value.reshape(rows.stop - rows.start, cap, width)

    def wait_for(part):
        for index in range(*part):
            if index < n_grp - 1:
                push(d_out.at[index], lying(index), g_send, g_recv.at[index], {"grp": grp}).wait_recv()

    for number, part in enumerate(parts[:-1]):
        wait_for(part)
        grad_rows(0, slot_total, part, number == 0, False, None)
    wait_for(parts[-1])
    only = len(parts) == 1
    grad_rows(0, hot_count, parts[-1], only, True, hot_done)

    per_half = hot_count // nc
    per_quarter = per_half // nx
    per_chip = per_quarter // ny

    def half_at(c):
        return pl.ds(pl.multiple_of(c * per_half, per_half), per_half)

    def quarter_at(x_):
        return pl.ds(pl.multiple_of(x_ * per_quarter, per_quarter), per_quarter)

    def chip_at(y_):
        return pl.ds(pl.multiple_of(y_ * per_chip, per_chip), per_chip)

    def total_quarter(x_):
        return pl.ds(pl.multiple_of(core * per_half + x_ * per_quarter, per_quarter), per_quarter)

    pair = push(hot_grad.at[half_at(1 - core)], pair_in, pair_sem.at[0], pair_sem.at[1], sibling)
    pair.start()
    grad_rows(hot_count, slot_total, parts[-1], only, True, cold_done)

    def cold_copy(other):
        return push(cold_grad.at[other], cold_in.at[me], c_sem.at[0], c_sem.at[1], {"wide": other})

    pair.wait()
    half[...] = (hot_grad[half_at(core), :].astype(F32) + pair_in[...].astype(F32)).astype(BF)
    for step in range(1, nx):
        to = lax.rem(x + step, nx)
        push(half.at[quarter_at(to)], x_in.at[x], xrs_sem.at[0], xrs_sem.at[1], at_wide(to, y)).start()
    x_in[x] = half[quarter_at(x), :]
    bytes_of(x_in.at[pl.ds(0, nx - 1)], xrs_sem).wait()
    quarter[...] = sum(x_in[x_].astype(F32) for x_ in range(nx)).astype(BF)
    for step in range(1, ny):
        to = lax.rem(y + step, ny)
        push(quarter.at[chip_at(to)], y_in.at[y], yrs_sem.at[0], yrs_sem.at[1], at_wide(x, to)).start()
    each(1, n_wide, lambda step: cold_copy(lax.rem(me + step, n_wide)).start())
    cold_in[me] = cold_grad[me]
    y_in[y] = quarter[chip_at(y), :]
    bytes_of(y_in.at[pl.ds(0, ny - 1)], yrs_sem).wait()
    mine = pl.ds(pl.multiple_of(core * per_half + x * per_quarter + y * per_chip, per_chip), per_chip)
    total_ref[mine, :] = sum(y_in[y_].astype(F32) for y_ in range(ny)).astype(BF)
    for step in range(1, ny):
        push(
            total_ref.at[mine], total_ref.at[mine], yag_sem.at[0], yag_sem.at[1], at_wide(x, lax.rem(y + step, ny))
        ).start()
    bytes_of(y_in.at[pl.ds(0, ny - 1)], yag_sem).wait()

    def to_sibling(x_):
        held = total_ref.at[total_quarter(x_)]
        return push(held, held, sib_send, sib_recv.at[x_], sibling)

    own = total_ref.at[total_quarter(x)]
    for step in range(1, nx):
        push(own, own, xag_send, xag_recv.at[x], at_wide(lax.rem(x + step, nx), y)).start()
    to_sibling(x).start()

    bytes_of(cold_in.at[pl.ds(0, n_wide - 1)], c_sem).wait()
    cold_sum_ref[...] = jnp.dot(
        chosen[...], cold_in[...].reshape(chosen.shape[1], LANES), preferred_element_type=F32
    )

    for step in range(1, nx):
        x_ = lax.rem(x + step, nx)
        held = total_ref.at[total_quarter(x_)]
        push(held, held, xag_send, xag_recv.at[x_], sibling).wait_recv()
        to_sibling(x_).start()
    for step in range(nx):
        to_sibling(lax.rem(x + step, nx)).wait_recv()
    sent = half.at[pl.ds(0, per_quarter * (nx - 1))]
    push(sent, sent, xag_send, xag_recv.at[0], sibling).wait_send()
    push(half, half, sib_send, sib_recv.at[0], sibling).wait_send()
    sent = d_out.at[pl.ds(0, n_grp - 1)]
    push(sent, sent, g_send, g_recv.at[0], sibling).wait_send()


def adagrad_kernel(
    logits_in, hot_grad, cold_grad, hot_ref, hot_accum, cold_ref, cold_accum,
    logits_ref, new_hot, new_hot_accum, new_cold, new_cold_accum,
):
    logits_ref[...] = logits_in[...]
    diagonal = (
        lax.broadcasted_iota(jnp.int32, (LANES, LANES), 0) == lax.broadcasted_iota(jnp.int32, (LANES, LANES), 1)
    )
    for grad_ref, rows_ref, accum_ref, new_rows, new_accum in (
        (hot_grad, hot_ref, hot_accum, new_hot, new_hot_accum),
        (cold_grad, cold_ref, cold_accum, new_cold, new_cold_accum),
    ):
        for start in range(0, rows_ref.shape[0], LANES):
            at = slice(start, start + LANES)
            gradient = grad_ref[at, :].astype(F32)
            old = jnp.sum(jnp.where(diagonal, accum_ref[:, at], 0.0), axis=1, keepdims=True)
            column = old + jnp.sum(gradient * gradient, axis=1, keepdims=True) / LANES
            new_accum[:, at] = jnp.sum(jnp.where(diagonal, column, 0.0), axis=0, keepdims=True)
            new_rows[at, :] = rows_ref[at, :] - gradient * (LEARN / (jnp.sqrt(column) + EPSILON))


VMEM = pl.BlockSpec(memory_space=pltpu.VMEM)
ANY = pl.BlockSpec(memory_space=pl.ANY)
DMA = pltpu.SemaphoreType.DMA


def on_device(
    n_wide, n_grp,
    dense_features, bag_slots, cold_offset, hot_rows, hot_accum, cold_rows, cold_accum,
    cross_down, cross_up, cross_bias, out_weight, labels,
):
    nx, ny, nc = wide_shape(n_wide)
    samples, width = dense_features.shape
    hot_count = hot_rows.shape[1]
    owned = cold_rows.shape[1]
    cap = cold_offset.shape[3]
    requests = n_wide * cap
    slot_total = hot_count + requests
    down_rows, rank = cross_down.shape
    up_rows, columns = cross_up.shape
    shard_rows = round_up(max(down_rows * rank, up_rows * columns) // LANES, 16)
    slots = jnp.transpose(bag_slots, (0, 2, 1))
    per_half = hot_count // nc
    per_quarter = per_half // nx

    def vm(*shape, dtype=BF):
        return pltpu.VMEM(shape, dtype)

    logits, hot_grad, cold_grad = pl.pallas_call(
        functools.partial(step_kernel, n_wide, n_grp),
        out_shape=(
            jax.ShapeDtypeStruct((1, samples), F32),
            jax.ShapeDtypeStruct((hot_count, width), BF),
            jax.ShapeDtypeStruct((owned, width), F32),
        ),
        in_specs=[VMEM, ANY, VMEM, VMEM, VMEM, ANY, VMEM, VMEM, VMEM, VMEM],
        out_specs=(VMEM,) * 3,
        scratch_shapes=[
            vm(owned, width, dtype=F32), vm(hot_count, width, dtype=F32), vm(1, 2 * columns + samples, dtype=F32),
            vm(LANES, LANES, dtype=F32), vm(n_wide, LANES, dtype=F32), vm(n_wide, LANES, dtype=F32),
            vm(requests // LANES, LANES, dtype=jnp.int32),
            vm(owned, width), vm(n_wide, cap, width), vm(n_wide, cap, width),
            vm(shard_rows, LANES, dtype=F32), vm(shard_rows, LANES), vm(shard_rows, LANES),
            vm(ny, nc, nx, shard_rows, LANES), vm(nx, nc, ny, shard_rows, LANES),
            vm(rank // LANES, columns, LANES, dtype=F32), vm(columns, rank), vm(rank, columns),
            vm(width, slot_total), vm(slot_total, n_grp * 2 * samples),
            vm(n_grp, width, 2 * samples, dtype=F32), vm(n_grp, samples, 2 * width),
            vm(samples, columns), vm(samples, columns, dtype=F32), vm(samples, rank),
            vm(n_grp, 2 * samples, width), vm(n_grp * 2 * samples, width), vm(slot_total, width, dtype=F32),
            vm(hot_count, width), vm(n_wide, cap, width), vm(n_wide, cap, width),
            vm(per_half, width), vm(per_half, width), vm(nx, per_quarter, width),
            vm(per_quarter, width), vm(ny, per_quarter // ny, width),
            vm(owned, requests),
        ]
        + [DMA((2,))] * 11
        + [DMA((3,)), DMA((ny,)), DMA((ny,)), DMA((ny,)), DMA((3,)), DMA((nx,)), DMA((nx,)), DMA((nx,))]
        + [DMA, DMA((n_grp,)), DMA, DMA((nx,)), DMA, DMA((nx,))],
        compiler_params=pltpu.CompilerParams(
            collective_id=0, has_side_effects=True, vmem_limit_bytes=60 * 1024 * 1024
        ),
        name="train_step",
    )(
        jnp.transpose(cold_offset[0, 0]), cold_rows[0], cross_down, cross_up, slots, hot_rows[0], dense_features,
        cross_bias, out_weight, labels,
    )

    steps = 2 if hot_count % (2 * LANES) == 0 and owned % (2 * LANES) == 0 else 1
    hot_block, cold_block = hot_count // steps, owned // steps

    def rows_spec(size):
        return pl.BlockSpec((size, width), lambda i: (i, 0))

    def accum_spec(size):
        return pl.BlockSpec((1, size), lambda i: (0, i))

    whole = pl.BlockSpec((1, samples), lambda i: (0, 0))
    logits, new_hot, new_hot_accum, new_cold, new_cold_accum = pl.pallas_call(
        adagrad_kernel,
        grid=(steps,),
        out_shape=(
            jax.ShapeDtypeStruct((1, samples), F32),
            jax.ShapeDtypeStruct((hot_count, width), F32),
            jax.ShapeDtypeStruct((1, hot_count), F32),
            jax.ShapeDtypeStruct((owned, width), F32),
            jax.ShapeDtypeStruct((1, owned), F32),
        ),
        in_specs=[
            whole, rows_spec(hot_block), rows_spec(cold_block),
            rows_spec(hot_block), accum_spec(hot_block), rows_spec(cold_block), accum_spec(cold_block),
        ],
        out_specs=(whole, rows_spec(hot_block), accum_spec(hot_block), rows_spec(cold_block), accum_spec(cold_block)),
        name="adagrad",
    )(logits, hot_grad, cold_grad, hot_rows[0], hot_accum, cold_rows[0], cold_accum)
    return (logits.reshape(samples), new_hot[None], new_hot_accum, new_cold[None], new_cold_accum)


def solution(mesh):
    return jax.shard_map(
        functools.partial(on_device, mesh.shape["wide"], mesh.shape["grp"]),
        mesh=mesh,
        in_specs=(
            P(("wide", "grp"), None),
            P("grp", "wide", None),
            P("grp", "wide", None, None),
            P("grp", None, None),
            P("grp", None),
            P("grp", "wide", None),
            P("grp", "wide"),
            P("wide", None),
            P("wide", None),
            P(),
            P(),
            P(("wide", "grp")),
        ),
        out_specs=(
            P(("wide", "grp")),
            P("grp", None, None),
            P("grp", None),
            P("grp", "wide", None),
            P("grp", "wide"),
        ),
        check_vma=False,
    )
```

```python
import functools

import jax
import jax.numpy as jnp
from jax import lax
from jax.experimental import pallas as pl
from jax.experimental.pallas import tpu as pltpu
from jax.sharding import PartitionSpec as P

LEARN = 0.1
EPSILON = 1e-08
LANES = 128
GRADIENT_TILE = 1024
GRADIENT_PARTS = {8: [(7, 8), (0, 3), (3, 7)], 2: [(1, 2), (0, 1)]}
BF = jnp.bfloat16
F32 = jnp.float32


def wide_shape(n_wide):
    return {64: (4, 8, 2), 16: (2, 4, 2), 8: (2, 2, 2)}[n_wide]


def round_up(value, unit):
    return -(-value // unit) * unit


def push(src, dst, send_sem, recv_sem, target):
    return pltpu.make_async_remote_copy(
        src_ref=src,
        dst_ref=dst,
        send_sem=send_sem,
        recv_sem=recv_sem,
        device_id=target,
        device_id_type=pl.DeviceIdType.MESH,
    )


def each(first, last, body):
    def step(i, carry):
        body(i)
        return carry

    lax.fori_loop(first, last, step, 0)


def far_first(count):
    return sorted(range(1, count), key=lambda o: -min(o, count - o)) + [0]


def step_kernel(
    n_wide, n_grp,
    offset_ref, cold_hbm, down_ref, up_ref, slots_ref, hot_hbm, dense_ref, bias_ref, head_ref, labels_ref,
    logits_ref, total_ref, cold_sum_hbm,
    cold_ref, hot_ref, small, square, ask, asked, asked_lane, cold_bf, picked, fetched,
    shard32, shard_down, shard_up, all_down, all_up, down32, down, up,
    buffer_t, counts, pooled_hot, pooled_out, stacked, gain, d_low, d_out, d_in, slot_grad,
    hot_grad, cold_grad, cold_in, pair_in, half, piece_in, far_in, cold_sum, chosen,
    load_sem, ask_sem, row_sem, d1_sem, u1_sem, p_sem, c_sem, pair_sem, prs_sem, far_sem,
    d_send, d_fwd, d_bwd, d_side, u_send, u_fwd, u_bwd, u_side, g_send, g_recv, back_send, back_recv, sib_send, sib_recv,
):
    nx, ny, nc = wide_shape(n_wide)
    chips = nx * ny
    me = lax.axis_index("wide")
    grp = lax.axis_index("grp")
    core = lax.rem(me, nc)
    chip = me // nc
    y = lax.rem(chip, ny)
    x = chip // ny
    sibling = {"wide": me + 1 - 2 * core}
    hot_count, width = hot_ref.shape
    owned = cold_ref.shape[0]
    cap = picked.shape[1]
    slot_total = buffer_t.shape[1]
    samples = dense_ref.shape[0]
    columns = stacked.shape[1]
    his = slot_total // LANES
    words = -(-his // 8)
    pool = slots_ref.shape[1]
    order = far_first(n_grp)

    def at_wide(x_, y_):
        return {"wide": (x_ * ny + y_) * nc + core}

    def bytes_of(ref, sems):
        return push(ref, ref, sems.at[0], sems.at[1], sibling)

    loads = [
        pltpu.make_async_copy(cold_hbm, cold_ref, load_sem.at[0]),
        pltpu.make_async_copy(hot_hbm, hot_ref, load_sem.at[1]),
    ]
    for load in loads:
        load.start()

    barrier = pltpu.get_barrier_semaphore()
    for axis, count, mine in (("wide", n_wide, me), ("grp", n_grp, grp)):
        each(1, count, lambda step: pl.semaphore_signal(
            barrier, inc=1, device_id={axis: lax.rem(mine + step, count)}, device_id_type=pl.DeviceIdType.MESH
        ))

    square[...] = jnp.zeros_like(square)
    square[:cap, :n_wide] = offset_ref[...].astype(F32)
    ask[...] = jnp.transpose(square[...])[:n_wide]
    for k in range(columns // LANES):
        at = slice(k * LANES, (k + 1) * LANES)
        small[:, at] = bias_ref[at].reshape(1, LANES)
        small[:, columns + k * LANES : columns + (k + 1) * LANES] = head_ref[at].astype(F32).reshape(1, LANES)
    small[:, 2 * columns :] = labels_ref[...].astype(F32).reshape(1, samples)
    down_rows, rank = down_ref.shape
    up_rows = up_ref.shape[0]
    shard32[...] = jnp.zeros_like(shard32)
    for j in range(rank // LANES):
        shard32[j * down_rows : (j + 1) * down_rows, :] = down_ref[:, j * LANES : (j + 1) * LANES].astype(F32)
    shard_down[...] = shard32[...].astype(BF)
    for j in range(columns // LANES):
        shard32[j * up_rows : (j + 1) * up_rows, :] = up_ref[:, j * LANES : (j + 1) * LANES].astype(F32)
    shard_up[...] = shard32[...].astype(BF)
    all_down[y, core, x] = shard_down[...]
    all_up[x, core, y] = shard_up[...]
    pl.semaphore_wait(barrier, n_wide + n_grp - 2)

    def row_of(index):
        return pl.ds(index, 1)

    def ask_copy(other):
        return push(ask.at[row_of(other)], asked.at[row_of(me)], ask_sem.at[0], ask_sem.at[1], {"wide": other})

    each(1, n_wide, lambda step: ask_copy(lax.rem(me + step, n_wide)).start())
    asked[row_of(me), :] = ask[row_of(me), :]

    for step in far_first(nx)[:-1]:
        push(
            shard_down, all_down.at[y, core, x], d1_sem.at[0], d1_sem.at[1], at_wide(lax.rem(x + step, nx), y)
        ).start()
    for step in far_first(ny)[:-1]:
        push(
            shard_up, all_up.at[x, core, y], u1_sem.at[0], u1_sem.at[1], at_wide(x, lax.rem(y + step, ny))
        ).start()

    def ring(blocks, mine, length, place, send, fwd_recv, bwd_recv, side_recv):
        n_fwd, n_bwd = length // 2, (length - 1) // 2

        def index(step):
            return lax.rem(mine + length - step, length)

        def fwd(step):
            held = blocks.at[index(step), core]
            return push(held, held, send.at[0], fwd_recv.at[step], place(lax.rem(mine + 1, length)))

        def bwd(step):
            held = blocks.at[lax.rem(mine + step, length), core]
            return push(held, held, send.at[1], bwd_recv.at[step], place(lax.rem(mine + length - 1, length)))

        def side(step):
            held = blocks.at[index(step), core]
            return push(held, held, send.at[2], side_recv.at[step], sibling)

        def start():
            fwd(0).start()
            if n_bwd:
                bwd(0).start()
            side(0).start()

        def serve(step):
            fwd(step).wait_recv()
            if step + 1 < n_fwd:
                fwd(step + 1).start()
            side(step + 1).start()
            if step < n_bwd:
                bwd(step).wait_recv()
                if step + 1 < n_bwd:
                    bwd(step + 1).start()
                side(length - step - 1).start()

        def ready(step):
            side(step).wait_recv()
            return index(step)

        def drain():
            for which, count in enumerate((n_fwd, n_bwd, length)):
                if count:
                    held = blocks.at[pl.ds(0, count), core]
                    push(held, held, send.at[which], side_recv.at[0], sibling).wait_send()

        steps = [[0]] + [[step + 1] + ([length - step - 1] if step < n_bwd else []) for step in range(n_fwd)]
        return start, serve, ready, drain, steps

    down_start, down_serve, down_ready, down_drain, down_steps = ring(
        all_down, y, ny, lambda row: at_wide(x, row), d_send, d_fwd, d_bwd, d_side
    )
    up_start, up_serve, up_ready, up_drain, up_steps = ring(
        all_up, x, nx, lambda row: at_wide(row, y), u_send, u_fwd, u_bwd, u_side
    )

    def down_rows_of(row):
        def shard(i):
            x_, c = i // nc, lax.rem(i, nc)
            shard32[...] = all_down[row, c, x_].astype(F32)
            first = ((x_ * ny + row) * nc + c) * down_rows
            for j in range(rank // LANES):
                down32[j, pl.ds(first, down_rows), :] = shard32[j * down_rows : (j + 1) * down_rows, :]

        each(0, nx * nc, shard)

    def up_rows_of(x_):
        def pair_of(y_):
            both = [all_up[x_, c, y_].astype(F32) for c in range(nc)]
            first = pl.multiple_of((x_ * ny + y_) * nc * up_rows, nc * up_rows)
            for j in range(columns // LANES):
                up[pl.ds(first, nc * up_rows), j * LANES : (j + 1) * LANES] = jnp.concatenate(
                    [part[j * up_rows : (j + 1) * up_rows] for part in both], axis=0
                ).astype(BF)

        each(0, ny, pair_of)

    def serve_down(step):
        if step < len(down_steps) - 1:
            down_serve(step)

    def serve_up(step):
        if step < len(up_steps) - 1:
            up_serve(step)

    def lay_down(step):
        for block in down_steps[step] if step < len(down_steps) else []:
            down_rows_of(down_ready(block))

    def lay_up(step):
        for block in up_steps[step] if step < len(up_steps) else []:
            up_rows_of(up_ready(block))

    def chunk_of(index):
        return lax.rem(grp + order[index], n_grp)

    def lanes_of(first, last):
        return slice(first * 2 * samples, last * 2 * samples)

    def count_chunk(index):
        chunk = chunk_of(index)
        at = pl.ds(pl.multiple_of(chunk * samples, LANES), samples)
        slots = jnp.concatenate([slots_ref[0, :, at], slots_ref[1, :, at]], axis=1)
        low = lax.bitwise_and(slots, LANES - 1)
        high = lax.shift_right_logical(slots, 7)
        unit = lax.shift_left(jnp.ones_like(high), 4 * lax.bitwise_and(high, 7))
        parts = [jnp.where(lax.shift_right_logical(high, 3) == k, unit, 0) for k in range(words)]

        def rows_step(q):
            ids = lax.broadcasted_iota(jnp.int32, (16, 2 * samples), 0) + q * 16
            total = [jnp.zeros((16, 2 * samples), jnp.int32) for _ in range(words)]
            for l in range(pool):
                hit = ids == low[l : l + 1, :]
                for k in range(words):
                    total[k] = total[k] + jnp.where(hit, parts[k][l : l + 1, :], 0)
            for h in range(his):
                digit = lax.bitwise_and(lax.shift_right_logical(total[h // 8], 4 * (h % 8)), 15)
                counts[pl.ds(pl.multiple_of(h * LANES + q * 16, 16), 16), lanes_of(index, index + 1)] = digit.astype(F32).astype(BF)

        each(0, LANES // 16, rows_step)

    def hot_pool(index):
        pooled_hot[index] = jnp.dot(
            buffer_t[:, :hot_count], counts[:hot_count, lanes_of(index, index + 1)], preferred_element_type=F32
        )

    early = (3 * n_grp) // 8
    for index in range(early):
        count_chunk(index)
    loads[0].wait()
    cold_bf[...] = cold_ref[...].astype(BF)
    bytes_of(all_down.at[y, core, pl.ds(0, nx - 1)], d1_sem).wait()
    down_start()

    asks = bytes_of(ask.at[pl.ds(0, n_wide - 1)], ask_sem)
    asks.wait_recv()
    per_batch = LANES // cap

    batches = n_wide // per_batch

    def batch_step(step):
        batch = lax.rem(me // per_batch + step, batches)
        spread = jnp.concatenate(
            [jnp.broadcast_to(asked[row_of(batch * per_batch + k), :], (cap, LANES)) for k in range(per_batch)], axis=0
        )
        lane = lax.broadcasted_iota(jnp.int32, (LANES, LANES), 1)
        row = lax.broadcasted_iota(jnp.int32, (LANES, LANES), 0)
        kept = jnp.where(lane == lax.rem(row, cap), spread, 0.0)
        wanted = jnp.sum(kept, axis=1, keepdims=True).astype(jnp.int32)
        asked_lane[pl.ds(batch, 1), :] = jnp.sum(jnp.transpose(kept), axis=0, keepdims=True).astype(jnp.int32)
        hit = lax.broadcasted_iota(jnp.int32, (LANES, owned), 1) == wanted
        rows = jnp.dot(jnp.where(hit, 1.0, 0.0).astype(BF), cold_bf[...], preferred_element_type=F32).astype(BF)
        for k in range(per_batch):
            other = batch * per_batch + k
            picked[other] = rows[k * cap : (k + 1) * cap]

            @pl.when(other != me)
            def _():
                push(
                    picked.at[other], fetched.at[me], row_sem.at[0], row_sem.at[1], {"wide": other}
                ).start()

    each(0, batches, batch_step)
    fetched[me] = picked[me]
    bytes_of(all_up.at[x, core, pl.ds(0, ny - 1)], u1_sem).wait()
    up_start()
    serve_down(0)

    stacked[:, :width] = dense_ref[...]
    loads[1].wait()
    for k in range(hot_count // LANES):
        buffer_t[:, k * LANES : (k + 1) * LANES] = jnp.transpose(hot_ref[k * LANES : (k + 1) * LANES, :]).astype(BF)
    for index in range(n_grp):
        if index >= early:
            count_chunk(index)
        hot_pool(index)

    def fill(batch):
        ids = lax.broadcasted_iota(jnp.int32, (owned, LANES), 0)
        chosen[:, pl.ds(pl.multiple_of(batch * LANES, LANES), LANES)] = jnp.where(
            ids == asked_lane[pl.ds(batch, 1), :], 1.0, 0.0
        ).astype(BF)

    asks.wait_send()
    rows_moved = bytes_of(picked.at[pl.ds(0, n_wide - 1)], row_sem)
    rows_moved.wait_recv()
    serve_down(1)
    serve_up(0)
    for k in range((slot_total - hot_count) // LANES):
        part = jnp.concatenate([fetched[k * per_batch + i] for i in range(per_batch)], axis=0).astype(F32)
        at = hot_count + k * LANES
        buffer_t[:, at : at + LANES] = jnp.transpose(part).astype(BF)

    def table_lanes(owner):
        return pl.ds(pl.multiple_of(width + 2 * width * owner, LANES), 2 * width)

    for index in range(n_grp):
        chunk = chunk_of(index)
        pooled_t = pooled_hot[index] + jnp.dot(
            buffer_t[:, hot_count:], counts[hot_count:, lanes_of(index, index + 1)], preferred_element_type=F32
        )
        for t in range(2):
            pooled_out[chunk, :, t * width : (t + 1) * width] = jnp.transpose(
                pooled_t[:, t * samples : (t + 1) * samples]
            ).astype(BF)
        if index < n_grp - 1:
            push(
                pooled_out.at[chunk], stacked.at[:, table_lanes(grp)], p_sem.at[0], p_sem.at[1], {"grp": chunk}
            ).start()
    stacked[:, table_lanes(grp)] = pooled_out[grp]

    serve_down(2)
    for step in range(len(down_steps)):
        if step == 1:
            serve_down(3)
        if step == len(down_steps) - 2:
            each(0, chosen.shape[1] // LANES, fill)
        serve_up(step + 1)
        lay_up(step)
        lay_down(step)
    up_drain()
    down_drain()

    def down_round(i):
        at = pl.ds(pl.multiple_of(i * LANES, LANES), LANES)
        for j in range(rank // LANES):
            down[at, j * LANES : (j + 1) * LANES] = down32[j, at, :].astype(BF)

    each(0, columns // LANES, down_round)
    rows_moved.wait_send()
    bytes_of(stacked.at[:, width : width + 2 * width * (n_grp - 1)], p_sem).wait()

    def bias_at(at):
        return small[:, at]

    def head_at(start, size):
        if isinstance(start, int):
            return small[:, columns + start : columns + start + size]
        return small[:, pl.ds(pl.multiple_of(columns + start, LANES), size)]

    low_rank = jnp.dot(stacked[...], down[...], preferred_element_type=F32).astype(BF)
    partial = jnp.zeros((samples, LANES), F32)
    for k in range(columns // LANES):
        at = slice(k * LANES, (k + 1) * LANES)
        wide = stacked[:, at].astype(F32)
        part = jnp.dot(low_rank, up[:, at], preferred_element_type=F32) + bias_at(at)
        gain[:, at] = part
        partial = partial + (wide * part + wide) * head_at(k * LANES, LANES)
    logits = jnp.sum(jnp.transpose(partial), axis=0, keepdims=True)
    logits_ref[...] = logits
    residual = jax.nn.sigmoid(logits) - small[:, 2 * columns :]
    residual = jnp.transpose(jnp.broadcast_to(residual, (LANES, samples)))
    low_grad = jnp.zeros((samples, rank), F32)
    for k in range(columns // LANES):
        at = slice(k * LANES, (k + 1) * LANES)
        d_crossed = residual * head_at(k * LANES, LANES)
        d_gain = (d_crossed * stacked[:, at].astype(F32)).astype(BF)
        low_grad = low_grad + lax.dot_general(
            d_gain, up[:, at], (((1,), (1,)), ((), ())), preferred_element_type=F32
        )
    d_low[...] = low_grad.astype(BF)

    def place_of(index):
        return order.index((n_grp - order[index]) % n_grp)

    def lying(index):
        return d_in.at[pl.ds(index * 2 * samples, 2 * samples)]

    for index in range(n_grp):
        other = chunk_of(index)
        at = table_lanes(other)
        back = lax.dot_general(
            d_low[...], down[at, :], (((1,), (1,)), ((), ())), preferred_element_type=F32
        )
        d_crossed = jnp.concatenate([residual, residual], axis=1) * head_at(width + 2 * width * other, 2 * width)
        d_both = (d_crossed * (gain[:, at] + 1.0) + back).astype(BF)
        if index < n_grp - 1:
            place = place_of(index)
            d_out[index, :samples] = d_both[:, :width]
            d_out[index, samples:] = d_both[:, width:]
            push(d_out.at[index], lying(place), g_send, g_recv.at[place], {"grp": other}).start()
        else:
            d_in[index * 2 * samples : index * 2 * samples + samples] = d_both[:, :width]
            d_in[index * 2 * samples + samples :] = d_both[:, width:]

    parts = GRADIENT_PARTS[n_grp]

    def grad_rows(start, stop, part, first, last, out):
        def tile_step(at):
            lanes = lanes_of(*part)
            total = jnp.dot(counts[at, lanes], d_in[lanes, :], preferred_element_type=F32)
            if not first:
                total = slot_grad[at, :] + total
            if last:
                out(at, total.astype(BF))
            else:
                slot_grad[at, :] = total

        for begin in range(start, stop, GRADIENT_TILE):
            tile_step(slice(begin, min(stop, begin + GRADIENT_TILE)))

    def hot_done(at, value):
        hot_grad[at, :] = value

    def cold_done(at, value):
        rows = slice((at.start - hot_count) // cap, (at.stop - hot_count) // cap)
        cold_grad[rows] = value.reshape(rows.stop - rows.start, cap, width)

    def wait_for(part):
        for index in range(*part):
            if index < n_grp - 1:
                push(d_out.at[index], lying(index), g_send, g_recv.at[index], {"grp": grp}).wait_recv()

    for number, part in enumerate(parts[:-1]):
        wait_for(part)
        grad_rows(0, slot_total, part, number == 0, False, None)
    wait_for(parts[-1])
    only = len(parts) == 1
    grad_rows(0, hot_count, parts[-1], only, True, hot_done)

    per_half = hot_count // nc
    members = nx * 2
    per_piece = per_half // members
    pairs = ny // 2
    pair_row, low_row = y // 2, lax.rem(y, 2)
    mine = x * 2 + low_row

    def half_at(c):
        return pl.ds(pl.multiple_of(c * per_half, per_half), per_half)

    def piece_at(k):
        return pl.ds(pl.multiple_of(k * per_piece, per_piece), per_piece)

    def total_at(k):
        return total_ref.at[pl.ds(pl.multiple_of(core * per_half + k * per_piece, per_piece), per_piece)]

    def member(k):
        return at_wide(k // 2, pair_row * 2 + lax.rem(k, 2))

    pair = push(hot_grad.at[half_at(1 - core)], pair_in, pair_sem.at[0], pair_sem.at[1], sibling)
    pair.start()
    grad_rows(hot_count, slot_total, parts[-1], only, True, cold_done)

    def cold_copy(other):
        return push(cold_grad.at[other], cold_in.at[me], c_sem.at[0], c_sem.at[1], {"wide": other})

    pair.wait()
    half[...] = (hot_grad[half_at(core), :].astype(F32) + pair_in[...].astype(F32)).astype(BF)
    for step in range(1, members):
        to = lax.rem(mine + step, members)
        push(half.at[piece_at(to)], piece_in.at[mine], prs_sem.at[0], prs_sem.at[1], member(to)).start()
    piece_in[mine] = half[piece_at(mine), :]
    bytes_of(piece_in.at[pl.ds(0, members - 1)], prs_sem).wait()
    far_in[pair_row] = sum(piece_in[k].astype(F32) for k in range(members)).astype(BF)
    held = far_in.at[pair_row]
    for step in range(1, pairs):
        to = at_wide(x, lax.rem(pair_row + step, pairs) * 2 + low_row)
        push(held, held, far_sem.at[0], far_sem.at[1], to).start()
    each(1, n_wide, lambda step: cold_copy(lax.rem(me + step, n_wide)).start())
    cold_in[me] = cold_grad[me]
    if pairs > 1:
        bytes_of(far_in.at[pl.ds(0, pairs - 1)], far_sem).wait()
    total_at(mine)[...] = sum(far_in[k].astype(F32) for k in range(pairs)).astype(BF)

    def to_sibling(k):
        return push(total_at(k), total_at(k), sib_send, sib_recv.at[k], sibling)

    for step in range(1, members):
        push(total_at(mine), total_at(mine), back_send, back_recv.at[mine], member(lax.rem(mine + step, members))).start()
    to_sibling(mine).start()

    bytes_of(cold_in.at[pl.ds(0, n_wide - 1)], c_sem).wait()
    cold_sum[...] = jnp.dot(
        chosen[...], cold_in[...].reshape(chosen.shape[1], LANES), preferred_element_type=F32
    )
    cold_out = pltpu.make_async_copy(cold_sum, cold_sum_hbm, load_sem.at[0])
    cold_out.start()

    for step in range(1, members):
        k = lax.rem(mine + step, members)
        push(total_at(k), total_at(k), back_send, back_recv.at[k], sibling).wait_recv()
        to_sibling(k).start()
    for step in range(members):
        to_sibling(lax.rem(mine + step, members)).wait_recv()
    sent = half.at[pl.ds(0, per_piece * (members - 1))]
    push(sent, sent, back_send, back_recv.at[0], sibling).wait_send()
    push(half, half, sib_send, sib_recv.at[0], sibling).wait_send()
    sent = d_out.at[pl.ds(0, n_grp - 1)]
    push(sent, sent, g_send, g_recv.at[0], sibling).wait_send()
    cold_out.wait()


def adagrad_kernel(
    logits_in, hot_grad, cold_grad, hot_ref, hot_accum, cold_ref, cold_accum,
    logits_ref, new_hot, new_hot_accum, new_cold, new_cold_accum,
):
    logits_ref[...] = logits_in[...]
    diagonal = (
        lax.broadcasted_iota(jnp.int32, (LANES, LANES), 0) == lax.broadcasted_iota(jnp.int32, (LANES, LANES), 1)
    )
    for grad_ref, rows_ref, accum_ref, new_rows, new_accum in (
        (hot_grad, hot_ref, hot_accum, new_hot, new_hot_accum),
        (cold_grad, cold_ref, cold_accum, new_cold, new_cold_accum),
    ):
        for start in range(0, rows_ref.shape[0], LANES):
            at = slice(start, start + LANES)
            gradient = grad_ref[at, :].astype(F32)
            old = jnp.sum(jnp.where(diagonal, accum_ref[:, at], 0.0), axis=1, keepdims=True)
            column = old + jnp.sum(gradient * gradient, axis=1, keepdims=True) / LANES
            new_accum[:, at] = jnp.sum(jnp.where(diagonal, column, 0.0), axis=0, keepdims=True)
            new_rows[at, :] = rows_ref[at, :] - gradient * (LEARN / (jnp.sqrt(column) + EPSILON))


VMEM = pl.BlockSpec(memory_space=pltpu.VMEM)
ANY = pl.BlockSpec(memory_space=pl.ANY)
DMA = pltpu.SemaphoreType.DMA


def on_device(
    n_wide, n_grp,
    dense_features, bag_slots, cold_offset, hot_rows, hot_accum, cold_rows, cold_accum,
    cross_down, cross_up, cross_bias, out_weight, labels,
):
    nx, ny, nc = wide_shape(n_wide)
    samples, width = dense_features.shape
    hot_count = hot_rows.shape[1]
    owned = cold_rows.shape[1]
    cap = cold_offset.shape[3]
    requests = n_wide * cap
    slot_total = hot_count + requests
    down_rows, rank = cross_down.shape
    up_rows, columns = cross_up.shape
    shard_rows = round_up(max(down_rows * rank, up_rows * columns) // LANES, 16)
    slots = jnp.transpose(bag_slots, (0, 2, 1))
    per_half = hot_count // nc
    members = nx * 2

    def vm(*shape, dtype=BF):
        return pltpu.VMEM(shape, dtype)

    logits, hot_grad, cold_grad = pl.pallas_call(
        functools.partial(step_kernel, n_wide, n_grp),
        out_shape=(
            jax.ShapeDtypeStruct((1, samples), F32),
            jax.ShapeDtypeStruct((hot_count, width), BF),
            jax.ShapeDtypeStruct((owned, width), F32),
        ),
        in_specs=[VMEM, ANY, VMEM, VMEM, VMEM, ANY, VMEM, VMEM, VMEM, VMEM],
        out_specs=(VMEM, VMEM, ANY),
        scratch_shapes=[
            vm(owned, width, dtype=F32), vm(hot_count, width, dtype=F32), vm(1, 2 * columns + samples, dtype=F32),
            vm(LANES, LANES, dtype=F32), vm(n_wide, LANES, dtype=F32), vm(n_wide, LANES, dtype=F32),
            vm(requests // LANES, LANES, dtype=jnp.int32),
            vm(owned, width), vm(n_wide, cap, width), vm(n_wide, cap, width),
            vm(shard_rows, LANES, dtype=F32), vm(shard_rows, LANES), vm(shard_rows, LANES),
            vm(ny, nc, nx, shard_rows, LANES), vm(nx, nc, ny, shard_rows, LANES),
            vm(rank // LANES, columns, LANES, dtype=F32), vm(columns, rank), vm(rank, columns),
            vm(width, slot_total), vm(slot_total, n_grp * 2 * samples),
            vm(n_grp, width, 2 * samples, dtype=F32), vm(n_grp, samples, 2 * width),
            vm(samples, columns), vm(samples, columns, dtype=F32), vm(samples, rank),
            vm(n_grp, 2 * samples, width), vm(n_grp * 2 * samples, width), vm(slot_total, width, dtype=F32),
            vm(hot_count, width), vm(n_wide, cap, width), vm(n_wide, cap, width),
            vm(per_half, width), vm(per_half, width), vm(members, per_half // members, width),
            vm(ny // 2, per_half // members, width), vm(owned, width, dtype=F32), vm(owned, requests),
        ]
        + [DMA((2,))] * 10
        + [DMA((3,)), DMA((ny,)), DMA((ny,)), DMA((ny,)), DMA((3,)), DMA((nx,)), DMA((nx,)), DMA((nx,))]
        + [DMA, DMA((n_grp,)), DMA, DMA((members,)), DMA, DMA((members,))],
        compiler_params=pltpu.CompilerParams(
            collective_id=0, has_side_effects=True, vmem_limit_bytes=60 * 1024 * 1024
        ),
        name="train_step",
    )(
        jnp.transpose(cold_offset[0, 0]), cold_rows[0], cross_down, cross_up, slots, hot_rows[0], dense_features,
        cross_bias, out_weight, labels,
    )

    steps = 2 if hot_count % (2 * LANES) == 0 and owned % (2 * LANES) == 0 else 1
    hot_block, cold_block = hot_count // steps, owned // steps

    def rows_spec(size):
        return pl.BlockSpec((size, width), lambda i: (i, 0))

    def accum_spec(size):
        return pl.BlockSpec((1, size), lambda i: (0, i))

    whole = pl.BlockSpec((1, samples), lambda i: (0, 0))
    logits, new_hot, new_hot_accum, new_cold, new_cold_accum = pl.pallas_call(
        adagrad_kernel,
        grid=(steps,),
        out_shape=(
            jax.ShapeDtypeStruct((1, samples), F32),
            jax.ShapeDtypeStruct((hot_count, width), F32),
            jax.ShapeDtypeStruct((1, hot_count), F32),
            jax.ShapeDtypeStruct((owned, width), F32),
            jax.ShapeDtypeStruct((1, owned), F32),
        ),
        in_specs=[
            whole, rows_spec(hot_block), rows_spec(cold_block),
            rows_spec(hot_block), accum_spec(hot_block), rows_spec(cold_block), accum_spec(cold_block),
        ],
        out_specs=(whole, rows_spec(hot_block), accum_spec(hot_block), rows_spec(cold_block), accum_spec(cold_block)),
        name="adagrad",
    )(logits, hot_grad, cold_grad, hot_rows[0], hot_accum, cold_rows[0], cold_accum)
    return (logits.reshape(samples), new_hot[None], new_hot_accum, new_cold[None], new_cold_accum)


def solution(mesh):
    return jax.shard_map(
        functools.partial(on_device, mesh.shape["wide"], mesh.shape["grp"]),
        mesh=mesh,
        in_specs=(
            P(("wide", "grp"), None),
            P("grp", "wide", None),
            P("grp", "wide", None, None),
            P("grp", None, None),
            P("grp", None),
            P("grp", "wide", None),
            P("grp", "wide"),
            P("wide", None),
            P("wide", None),
            P(),
            P(),
            P(("wide", "grp")),
        ),
        out_specs=(
            P(("wide", "grp")),
            P("grp", None, None),
            P("grp", None),
            P("grp", "wide", None),
            P("grp", "wide"),
        ),
        check_vma=False,
    )
```
